128 devices in a mesh: gx: 8 (over z, y_hi), gy: 4 (over x), gz: 4 (over y_lo, core).
Axes of the slice: x: 4, y: 4 (y_hi: 2, y_lo: 2; y = y_hi * 2 + y_lo), z: 4, core: 2. Of those that a mesh axis runs over, the one named last changes fastest.
Arguments:
- coarse_in: bfloat16 [32, 32, 2048], P('gx', 'gy', 'gz'), may hold values from -6 to 6
- out_grad: bfloat16 [64, 64, 4096], P('gx', 'gy', 'gz'), may hold values from -6 to 6
- up_weight: bfloat16 [64, 64, 64], replicated, may hold values from -0.25 to 0.25
- conv_weight: bfloat16 [27, 64, 64], replicated, may hold values from -0.15625 to 0.15625
Outputs:
- grad_coarse: bfloat16 [32, 32, 2048], P('gx', 'gy', 'gz')
- grad_up: float32 [64, 64, 64], replicated
- grad_conv: float32 [27, 64, 64], replicated
The draws below stay inside these ranges and needn't reach their ends.
All inputs are finite; a program needn't handle non-finite values.
Results may differ from the reference program's by a relative error of at most 0.005.
Values may be sent and summed in bfloat16 or wider, within the bound.
A program may use at most 64 MiB of HBM per device.

```python
import jax
import jax.numpy as jnp
from jax import lax

C = 64
NX = 64
NY = 64
NZ = 64


def shard_levels(stream_key, dims, pieces, least, largest):
    level, own = 1.0, jax.random.fold_in(stream_key, 6)
    for axis_at, blocks in pieces:
        draws = jnp.exp(jax.random.uniform(jax.random.fold_in(own, axis_at), (blocks,), jnp.float32, least / len(pieces), largest / len(pieces)))
        level = level * jnp.repeat(draws, dims[axis_at] // blocks).reshape([-1 if axis == axis_at else 1 for axis in range(len(dims))])
    return level


def gaussian(rng, extent, scale, bound, pieces=(), kind=jnp.bfloat16):
    entries = jax.random.normal(rng, extent, jnp.float32) * scale
    if len(pieces) > 0:
        entries = shard_levels(rng, extent, pieces, -0.22, 0.18) * entries
    return jnp.clip(entries, min=-bound, max=bound).astype(kind)


def setup_inputs(seed: int = 0) -> dict:
    streams_of = jax.random.split(jax.random.key(seed), 5)
    return {
        "coarse_in": gaussian(streams_of[0], (NX // 2, NY // 2, NZ // 2 * C), 1.0, 6.0, ((0, 8), (1, 4), (2, 4))),
        "out_grad": gaussian(streams_of[1], (NX, NY, NZ * C), 1.0, 6.0, ((0, 8), (1, 4), (2, 4))),
        "up_weight": gaussian(streams_of[2], (64, C, C), (8 * C) ** -0.5, 0.25),
        "conv_weight": gaussian(streams_of[3], (27, C, C), (27 * C) ** -0.5, 0.15625),
    }


gelu_coef = 0.7978845608
gelu_cube = 0.044715
taps_by_parity = (((0, 3), (1, 1)), ((1, 2), (2, 0)))

def smooth_gate(value):
    inner = gelu_coef * (value + gelu_cube * value ** 3)
    return 0.5 * value * (1.0 + jnp.tanh(inner))

def gate_slope(value):
    tangent = jnp.tanh(gelu_coef * (value + gelu_cube * value ** 3))
    return 0.5 * (1.0 + tangent) + 0.5 * value * (1.0 - tangent * tangent) * gelu_coef * (1.0 + 3.0 * gelu_cube * value * value)

def parity_terms():
    listing = []
    for first in range(2):
        for second in range(2):
            for third in range(2):
                terms = []
                for shift_x, kern_x in taps_by_parity[first]:
                    for shift_y, kern_y in taps_by_parity[second]:
                        for shift_z, kern_z in taps_by_parity[third]:
                            terms.append(((shift_x, shift_y, shift_z), kern_x * 16 + kern_y * 4 + kern_z))
                listing.append(((first, second, third), terms))
    return listing

def conv_offsets():
    return [(tap // 9, tap // 3 % 3, tap % 3) for tap in range(27)]

def contract_rows(left, right):
    return lax.dot_general(left, right, (((0,), (0,)), ((), ())), preferred_element_type=jnp.float32)

def contract_cols(left, right):
    return lax.dot_general(left, right, (((1,), (1,)), ((), ())), preferred_element_type=jnp.float32)

def reference(coarse_in, out_grad, up_weight, conv_weight):
    half_x, half_y, half_z = (NX // 2, NY // 2, NZ // 2)
    coarse = coarse_in.reshape(half_x, half_y, half_z, C)
    grads = out_grad.reshape(NX, NY, NZ, C)
    factor = 1.0 / jnp.sqrt(jnp.float32(NX * NY * NZ))
    blocks = []
    for parity, terms in parity_terms():
        total = jnp.zeros((half_x * half_y * half_z, C), jnp.float32)
        for offsets, kernel in terms:
            moved = jnp.roll(coarse, (1 - offsets[0], 1 - offsets[1], 1 - offsets[2]), (0, 1, 2)).reshape(-1, C)
            total = total + jnp.dot(moved, up_weight[kernel], preferred_element_type=jnp.float32)
        blocks.append(total.reshape(half_x, half_y, half_z, C))
    stacked = jnp.stack(blocks).reshape(2, 2, 2, half_x, half_y, half_z, C)
    pre_act = stacked.transpose(3, 0, 4, 1, 5, 2, 6).reshape(NX, NY, NZ, C)
    hidden = smooth_gate(pre_act).astype(jnp.bfloat16)
    flat_grad = grads.reshape(-1, C)
    conv_terms = []
    grad_hidden = jnp.zeros((NX * NY * NZ, C), jnp.float32)
    for tap, offsets in enumerate(conv_offsets()):
        moved = jnp.roll(hidden, (1 - offsets[0], 1 - offsets[1], 1 - offsets[2]), (0, 1, 2)).reshape(-1, C)
        conv_terms.append(contract_rows(moved, flat_grad))
        back = jnp.roll(grads, (offsets[0] - 1, offsets[1] - 1, offsets[2] - 1), (0, 1, 2)).reshape(-1, C)
        grad_hidden = grad_hidden + contract_cols(back, conv_weight[tap])
    grad_conv = jnp.stack(conv_terms) * factor
    grad_pre = (grad_hidden.reshape(NX, NY, NZ, C) * gate_slope(pre_act)).astype(jnp.bfloat16)
    pre_parts = grad_pre.reshape(half_x, 2, half_y, 2, half_z, 2, C)
    up_terms = [None] * 64
    total = jnp.zeros((half_x * half_y * half_z, C), jnp.float32)
    for parity, terms in parity_terms():
        part = pre_parts[:, parity[0], :, parity[1], :, parity[2], :]
        flat_part = part.reshape(-1, C)
        for offsets, kernel in terms:
            moved = jnp.roll(coarse, (1 - offsets[0], 1 - offsets[1], 1 - offsets[2]), (0, 1, 2)).reshape(-1, C)
            up_terms[kernel] = contract_rows(moved, flat_part)
            back = jnp.roll(part, (offsets[0] - 1, offsets[1] - 1, offsets[2] - 1), (0, 1, 2)).reshape(-1, C)
            total = total + contract_cols(back, up_weight[kernel])
    grad_up = jnp.stack(up_terms) * factor
    grad_coarse = total.astype(jnp.bfloat16).reshape(half_x, half_y, half_z * C)
    return (grad_coarse, grad_up, grad_conv)
```

```python
import functools
import itertools
import math

import jax
import jax.numpy as jnp
from jax import lax
from jax.experimental import pallas as pl
from jax.experimental.pallas import tpu as pltpu
from jax.sharding import PartitionSpec as P

MESH = pl.DeviceIdType.MESH
F32 = jnp.float32
BF16 = jnp.bfloat16
C = 64
gelu_coef = 0.7978845608
gelu_cube = 0.044715
taps_by_parity = (((0, 3), (1, 1)), ((1, 2), (2, 0)))
NEIGHBOURS = [o for o in itertools.product((-1, 0, 1), repeat=3) if any(o)]


def nt(left, right):
    return lax.dot_general(left, right, (((1,), (1,)), ((), ())), preferred_element_type=F32)


def nn(left, right):
    return jnp.dot(left, right, preferred_element_type=F32)


class Place:
    def __init__(self, sizes):
        self.sizes = sizes
        self.gx, self.gy, self.gz = (lax.axis_index(a) for a in ("gx", "gy", "gz"))
        self.nz, self.nx, self.ny = sizes[0] // 2, sizes[1], sizes[2]
        self.low = sizes[2] // 2
        self.z, self.x = self.gx // 2, self.gy
        self.y = self.gx % 2 * self.low + self.gz // 2
        self.core = self.gz % 2
        self.index = self.z * self.nx + self.x
        self.group = self.nz * self.nx
        self.row_group = 2 * self.low

    def neighbour(self, o):
        me = (self.gx, self.gy, self.gz)
        return tuple(lax.rem(m + d + n, n) for m, d, n in zip(me, o, self.sizes))

    def sibling(self):
        return (self.gx, self.gy, self.gz + 1 - 2 * self.core)

    def in_group(self, dz, dx):
        z, x = lax.rem(self.z + dz, self.nz), lax.rem(self.x + dx, self.nx)
        return (z * 2 + self.gx % 2, x, self.gz), z * self.nx + x

    def in_row(self, dy):
        y = lax.rem(self.y + dy, self.row_group)
        return (self.z * 2 + y // self.low, self.x, y % self.low * 2 + self.core)

    def group_steps(self):
        return [o for o in itertools.product(range(self.nz), range(self.nx)) if any(o)]


def remote(src, dst, send, recv, device):
    return pltpu.make_async_remote_copy(
        src_ref=src, dst_ref=dst, send_sem=send, recv_sem=recv, device_id=device, device_id_type=MESH
    )


def fine_halo(place, xt, ys, yt, send, recv):
    copies = []
    nx, lanes = xt.shape[0] - 2, xt.shape[2] - 256
    for i, (ox, oy, oz) in enumerate(NEIGHBOURS):
        zs, zd = {
            0: (pl.ds(0, lanes), pl.ds(128, lanes)),
            1: (pl.ds(lanes - 128, 128), pl.ds(0, 128)),
            -1: (pl.ds(0, 128), pl.ds(lanes + 128, 128)),
        }[oz]
        if oy == 0:
            zs = pl.ds(zs.start + 128, zs.size)
            xs, xd = {0: (pl.ds(1, nx), pl.ds(1, nx)), 1: (nx, 0), -1: (1, nx + 1)}[ox]
            src, dst = xt.at[xs, :, zs], xt.at[xd, :, zd]
        else:
            side = (1 - oy) // 2
            src, dst = ys.at[side, :, zs], yt.at[side, 1 - ox, :, zd]
        copies.append(remote(src, dst, send.at[i], recv.at[i], place.neighbour((ox, oy, oz))))
    for copy in copies:
        copy.start()
    return copies


def coarse_halo(place, ue, us, yt, send, recv):
    copies = []
    nx, lanes = ue.shape[0] - 2, ue.shape[2] - 256
    for i, (ox, oy, oz) in enumerate(NEIGHBOURS):
        zs, zd = {
            0: (pl.ds(0, lanes), pl.ds(128, lanes)),
            1: (pl.ds(lanes - 128, 128), pl.ds(0, 128)),
            -1: (pl.ds(0, 128), pl.ds(lanes + 128, 128)),
        }[oz]
        if oy == 0:
            zs = pl.ds(zs.start + 128, zs.size)
            xs, xd = {0: (pl.ds(1, nx), pl.ds(1, nx)), 1: (nx, 0), -1: (1, nx + 1)}[ox]
            src, dst = ue.at[xs, pl.ds(8, 8), zs], ue.at[xd, pl.ds(8, 8), zd]
        else:
            side = (1 - oy) // 2
            src, dst = us.at[side, :, zs], yt.at[side, 1 - ox, :, zd]
        copies.append(remote(src, dst, send.at[i], recv.at[i], place.neighbour((ox, oy, oz))))
    for copy in copies:
        copy.start()
    return copies


def fill_fine(xt, yt, yr, ge):
    nx, pairs = xt.shape[0] - 2, ge.shape[0]
    wide = 128 * pairs
    turn = xt.shape[2] - 64
    for side in range(2):
        for slot in range(3):
            yr[side, slot] = pltpu.roll(yt[side, slot], turn, 1)[:, :wide]
    for x in range(nx + 2):
        turned = pltpu.roll(xt[x].astype(F32), turn, 1)
        slot, row = (0, nx - 1) if x == 0 else (2, 0) if x == nx + 1 else (1, x - 1)
        for pair in range(pairs):
            lanes = slice(128 * pair, 128 * pair + 128)
            ge[pair, x, 8:24, :] = turned[:, lanes]
            ge[pair, x, 7:8, :] = yr[0, slot, row : row + 1, lanes]
            ge[pair, x, 24:25, :] = yr[1, slot, row : row + 1, lanes]


class AllReduce:
    def __init__(self, place, total, fin, r1, s, r2, r3, sems):
        self.place, self.total, self.fin = place, total, fin
        self.r1, self.s, self.r2, self.r3, self.sems = r1, s, r2, r3, sems
        self.half = total.shape[0] // 2
        self.piece = self.half // place.group
        self.used = 0
        self.flight = []

    def send(self, src, dst, device):
        i = self.used
        self.used += 1
        copy = remote(src, dst, self.sems.at[0, i], self.sems.at[1, i], device)
        copy.start()
        self.flight.append(copy)

    def arrive(self):
        for copy in self.flight:
            copy.wait()
        self.flight = []

    def mine(self, index, size):
        return pl.ds(pl.multiple_of(index * size, size), size)

    def pair(self):
        p = self.place
        self.send(self.total.at[self.mine(1 - p.core, self.half)], self.r1, p.sibling())

    def scatter(self):
        p = self.place
        self.arrive()
        self.s[...] = (self.total[self.mine(p.core, self.half), :] + self.r1[...]).astype(BF16)
        for k, o in enumerate(p.group_steps()):
            device, index = p.in_group(*o)
            self.send(self.s.at[self.mine(index, self.piece)], self.r2.at[k], device)

    def exchange(self):
        p = self.place
        self.arrive()
        total = self.s[self.mine(p.index, self.piece), :].astype(F32)
        for k in range(p.group - 1):
            total = total + self.r2[k].astype(F32)
        self.r3[p.y] = total.astype(BF16)
        for dy in range(1, p.row_group):
            self.send(self.r3.at[p.y], self.r3.at[p.y], p.in_row(dy))

    def spot(self):
        p = self.place
        return pl.ds(pl.multiple_of(p.core * self.half + p.index * self.piece, self.piece), self.piece)

    def gather(self):
        p = self.place
        self.arrive()
        total = self.r3[0].astype(F32)
        for k in range(1, p.row_group):
            total = total + self.r3[k].astype(F32)
        self.fin[self.spot(), :] = total.astype(BF16)
        for o in p.group_steps():
            device, _ = p.in_group(*o)
            self.send(self.fin.at[self.spot()], self.fin.at[self.spot()], device)

    def share(self):
        p = self.place
        self.arrive()
        spot = self.mine(p.core, self.half)
        self.send(self.fin.at[spot], self.fin.at[spot], p.sibling())


def main_kernel(
    sizes, u_in, g_in, wu_in, wc_in,
    coarse_out, fin_up, fin_conv,
    ub, wu, wc, ue, ue1, us, uyt, gxt, gf, ys, gyt, gyr, ge, gd,
    wp, cw, w3, uw, uwt, pre, slope, ht, gh, gp, pxt, pys, pyt, gc,
    a_up, a_conv, up_r1, up_s, up_r2, up_r3, cv_r1, cv_s, cv_r2, cv_r3,
    local_sems, u_sems, g_sems, p_sems, up_sems, cv_sems,
):
    place = Place(sizes)
    barrier = pltpu.get_barrier_semaphore()
    partners = [place.neighbour(o) for o in NEIGHBOURS]
    partners += [place.in_group(*o)[0] for o in place.group_steps()]
    partners += [place.in_row(dy) for dy in range(1, place.row_group)]
    partners += [place.sibling()]
    for device in partners:
        pl.semaphore_signal(barrier, inc=1, device_id=device, device_id_type=MESH)
    loads = [
        pltpu.make_async_copy(u_in, ub, local_sems.at[0]),
        pltpu.make_async_copy(g_in, gxt.at[pl.ds(1, 8), :, pl.ds(128, 1024)], local_sems.at[1]),
        pltpu.make_async_copy(wu_in, wu, local_sems.at[2]),
        pltpu.make_async_copy(wc_in, wc, local_sems.at[3]),
    ]
    for load in loads:
        load.start()

    loads[0].wait()
    for x in range(4):
        ue[1 + x, 8:16, 128:640] = ub[x].astype(F32)
    for x in range(4):
        us[0, x : x + 1, :] = ue[1 + x, 15:16, 128:640]
        us[1, x : x + 1, :] = ue[1 + x, 8:9, 128:640]
    us[0, 4:8, :] = jnp.zeros((4, 512), F32)
    us[1, 4:8, :] = jnp.zeros((4, 512), F32)
    loads[1].wait()
    for x in range(8):
        gf[x] = gxt[1 + x, :, 128:1152].astype(F32)
    for x in range(8):
        ys[0, x : x + 1, :] = gf[x, 15:16, :]
        ys[1, x : x + 1, :] = gf[x, 0:1, :]
    pl.semaphore_wait(barrier, len(partners))
    u_copies = coarse_halo(place, ue, us, uyt, u_sems.at[0], u_sems.at[1])
    g_copies = fine_halo(place, gxt, ys, gyt, g_sems.at[0], g_sems.at[1])

    loads[2].wait()
    loads[3].wait()
    blank = jnp.zeros((C, C), BF16)
    for q in range(16):
        k0, k1, k2, k3 = (wu[4 * q + k] for k in range(4))
        wp[q, 0:64, :] = jnp.concatenate([k3, blank], axis=1)
        wp[q, 64:128, :] = jnp.concatenate([k1, k2], axis=1)
        wp[q, 128:192, :] = jnp.concatenate([blank, k0], axis=1)
        wp[q, 192:256, :] = jnp.zeros((C, 2 * C), BF16)
        w3[q, :, 0:128] = jnp.concatenate([k0, k1], axis=1)
        w3[q, :, 128:256] = jnp.concatenate([k2, k3], axis=1)
    for t in range(9):
        d0, d1, d2 = (wc[3 * t + d] for d in range(3))
        cw[t, 0:64, 0:128] = jnp.concatenate([d2, d1], axis=1)
        cw[t, 0:64, 128:256] = jnp.concatenate([d0, blank], axis=1)
        cw[t, 64:128, 0:128] = jnp.concatenate([blank, d2], axis=1)
        cw[t, 64:128, 128:256] = jnp.concatenate([d1, d0], axis=1)

    for copy in u_copies:
        copy.wait()
    for x in range(6):
        slot, row = (0, 3) if x == 0 else (2, 0) if x == 5 else (1, x - 1)
        ue[x, 7:8, :] = uyt[0, slot, row : row + 1, :]
        ue[x, 16:17, :] = uyt[1, slot, row : row + 1, :]
    for x in range(6):
        ue1[x] = pltpu.roll(ue[x], 768 - 64, 1)[:, :640]
    for sx in range(3):
        for sy in range(3):
            rows = []
            for zc in range(8):
                if zc % 2:
                    part = ue[sx : sx + 4, 7 + sy : 15 + sy, 64 * (zc + 1) : 64 * (zc + 1) + 256]
                else:
                    part = ue1[sx : sx + 4, 7 + sy : 15 + sy, 64 * zc : 64 * zc + 256]
                rows.append(part.reshape(32, 256))
            window = jnp.concatenate(rows, axis=0)
            uw[3 * sx + sy] = window.astype(BF16)
            uwt[3 * sx + sy] = window.T.astype(BF16)[:192]

    for px in range(2):
        for py in range(2):
            total = None
            for sx, kx in taps_by_parity[px]:
                for sy, ky in taps_by_parity[py]:
                    part = nn(uw[3 * sx + sy], wp[4 * kx + ky])
                    total = part if total is None else total + part
            total = total.reshape(8, 4, 8, 128)
            for zc in range(8):
                for xc in range(4):
                    pre[zc, 2 * xc + px, pl.ds(py, 8, stride=2), :] = total[zc, xc]
    for zc in range(8):
        v = pre[zc].reshape(128, 128)
        square = v * v
        tangent = jnp.tanh(gelu_coef * (v + gelu_cube * (square * v)))
        hidden = 0.5 * v * (1.0 + tangent)
        ht[:, 128 * zc : 128 * zc + 128] = hidden.T.astype(BF16)
        slope[zc] = 0.5 * (1.0 + tangent) + 0.5 * v * (1.0 - tangent * tangent) * gelu_coef * (
            1.0 + 3.0 * gelu_cube * square
        )

    for copy in g_copies:
        copy.wait()
    fill_fine(gxt, gyt, gyr, ge)
    for x in range(10):
        for k in range(3):
            for pair in range(9):
                gd[k, x, :, 128 * pair : 128 * pair + 128] = ge[pair, x, 7 + k : 23 + k, :].astype(BF16)

    def windows(t):
        dx, dy = t // 3, t % 3
        parts = [
            gd[2 - dy, pl.ds(2 - dx, 8), :, 128 * zc : 128 * zc + 256].reshape(128, 256) for zc in range(8)
        ]
        return jnp.concatenate(parts, axis=0)

    gh[...] = jnp.zeros_like(gh)

    def hidden_step(t, carry):
        gh[...] += nt(windows(t), cw[t])
        return carry

    lax.fori_loop(0, 9, hidden_step, 0)
    for zc in range(8):
        grad = (gh[128 * zc : 128 * zc + 128, :] * slope[zc]).astype(BF16).reshape(8, 16, 128)
        pxt[1:9, :, 128 * zc + 128 : 128 * zc + 256] = grad
        gp[zc] = grad.astype(F32)
        for x in range(8):
            pys[0, x : x + 1, 128 * zc : 128 * zc + 128] = gp[zc, x, 15:16, :]
            pys[1, x : x + 1, 128 * zc : 128 * zc + 128] = gp[zc, x, 0:1, :]
    p_copies = fine_halo(place, pxt, pys, pyt, p_sems.at[0], p_sems.at[1])

    low = lax.broadcasted_iota(jnp.int32, (C, 2 * C), 1) < C
    for px in range(2):
        for py in range(2):
            rows = []
            for zc in range(8):
                for xc in range(4):
                    rows.append(gp[zc, 2 * xc + px, pl.ds(py, 8, stride=2), :])
            grad = jnp.concatenate(rows, axis=0).astype(BF16)
            for sx, kx in taps_by_parity[px]:
                for sy, ky in taps_by_parity[py]:
                    q = 4 * kx + ky
                    part = nn(uwt[3 * sx + sy], grad)
                    a_up[128 * q : 128 * q + 64, :] = part[64:128]
                    a_up[128 * q + 64 : 128 * q + 128, :] = jnp.where(low, part[0:64], part[128:192])
    up = AllReduce(place, a_up, fin_up, up_r1, up_s, up_r2, up_r3, up_sems)
    up.pair()

    def conv_step(t, carry):
        part = nn(ht[...], windows(t))
        gc[t] = part[:64] + pltpu.roll(part[64:], 256 - 64, 1)
        return carry

    lax.fori_loop(0, 4, conv_step, 0)
    up.scatter()
    lax.fori_loop(4, 9, conv_step, 0)
    for t in range(9):
        a_conv[64 * t : 64 * t + 64, :] = gc[t, :, 0:128]
    for m in range(5):
        if m < 4:
            other = pltpu.roll(gc[2 * m + 1, :, 128:256], 64, 1)
            joined = jnp.where(low, gc[2 * m, :, 128:256], other)
        else:
            joined = gc[8, :, 128:256]
        a_conv[64 * (9 + m) : 64 * (10 + m), :] = joined
    a_conv[896:1024, :] = jnp.zeros((128, 128), F32)
    conv = AllReduce(place, a_conv, fin_conv, cv_r1, cv_s, cv_r2, cv_r3, cv_sems)
    conv.pair()
    conv.scatter()
    up.exchange()

    for copy in p_copies:
        copy.wait()
    fill_fine(pxt, pyt, gyr, ge)
    total = None
    for kx in range(4):
        for ky in range(4):
            rows = []
            for zc in range(8):
                for xc in range(4):
                    rows.append(
                        jnp.concatenate(
                            [
                                ge[zc + s, 2 * xc + kx, pl.ds(7 + ky, 8, stride=2), :]
                                for s in range(2)
                            ],
                            axis=1,
                        )
                    )
            part = nt(jnp.concatenate(rows, axis=0).astype(BF16), w3[4 * kx + ky])
            total = part if total is None else total + part
        if kx == 1:
            up.gather()
            conv.exchange()
    total = total.reshape(8, 4, 8, C)
    for zc in range(0, 8, 2):
        coarse_out[:, :, 64 * zc : 64 * zc + 128] = jnp.concatenate(
            [total[zc], total[zc + 1]], axis=2
        ).astype(BF16)
    conv.gather()
    up.share()
    conv.share()
    up.arrive()
    conv.arrive()


def last_kernel(factor, coarse, fin_up, fin_conv, coarse_out, up_out, conv_out):
    coarse_out[...] = coarse[...]
    for q in range(16):
        first = fin_up[128 * q : 128 * q + 64, :].astype(F32) * factor
        second = fin_up[128 * q + 64 : 128 * q + 128, :].astype(F32) * factor
        up_out[4 * q + 1] = first[:, :C]
        up_out[4 * q + 2] = first[:, C:]
        up_out[4 * q + 3] = second[:, :C]
        up_out[4 * q] = second[:, C:]
    for t in range(9):
        both = fin_conv[64 * t : 64 * t + 64, :].astype(F32) * factor
        conv_out[3 * t + 2] = both[:, :C]
        conv_out[3 * t + 1] = both[:, C:]
        m = t // 2
        rest = fin_conv[64 * (9 + m) : 64 * (10 + m), :].astype(F32) * factor
        conv_out[3 * t] = rest[:, C:] if t % 2 else rest[:, :C]


def local(sizes, coarse_in, out_grad, up_weight, conv_weight):
    every_cell = 2048 * sizes[0] * sizes[1] * sizes[2]
    group = sizes[0] // 2 * sizes[1]
    row_group = sizes[2] // 2 * 2
    up_piece, cv_piece = 1024 // group, 512 // group
    messages = 2 + 2 * (group - 1) + row_group - 1
    vmem = pltpu.VMEM
    dma = pltpu.SemaphoreType.DMA
    whole = pl.BlockSpec(memory_space=vmem)
    anywhere = pl.BlockSpec(memory_space=pl.ANY)
    scratch = [
        vmem((4, 8, 512), BF16), vmem((64, C, C), BF16), vmem((27, C, C), BF16),
        vmem((6, 24, 768), F32), vmem((6, 24, 640), F32), vmem((2, 8, 512), F32), vmem((2, 3, 8, 768), F32),
        vmem((10, 16, 1280), BF16), vmem((8, 16, 1024), F32), vmem((2, 8, 1024), F32),
        vmem((2, 3, 8, 1280), F32), vmem((2, 3, 8, 1152), F32), vmem((9, 10, 32, 128), F32),
        vmem((3, 10, 16, 1152), BF16),
        vmem((16, 256, 128), BF16), vmem((9, 128, 256), BF16), vmem((16, 64, 256), BF16),
        vmem((9, 256, 256), BF16), vmem((9, 192, 256), BF16),
        vmem((8, 8, 16, 128), F32), vmem((8, 128, 128), F32), vmem((128, 1024), BF16), vmem((1024, 128), F32),
        vmem((8, 8, 16, 128), F32),
        vmem((10, 16, 1280), BF16), vmem((2, 8, 1024), F32), vmem((2, 3, 8, 1280), F32), vmem((9, 64, 256), F32),
        vmem((2048, 128), F32), vmem((1024, 128), F32),
        vmem((1024, 128), F32), vmem((1024, 128), BF16), vmem((group - 1, up_piece, 128), BF16),
        vmem((row_group, up_piece, 128), BF16),
        vmem((512, 128), F32), vmem((512, 128), BF16), vmem((group - 1, cv_piece, 128), BF16),
        vmem((row_group, cv_piece, 128), BF16),
        dma((4,)), dma((2, 26)), dma((2, 26)), dma((2, 26)), dma((2, messages)), dma((2, messages)),
    ]
    coarse, fin_up, fin_conv = pl.pallas_call(
        functools.partial(main_kernel, sizes),
        name="halo_compute_reduce",
        out_shape=(
            jax.ShapeDtypeStruct((4, 8, 512), BF16),
            jax.ShapeDtypeStruct((2048, 128), BF16),
            jax.ShapeDtypeStruct((1024, 128), BF16),
        ),
        in_specs=[anywhere] * 4,
        out_specs=(whole, whole, whole),
        scratch_shapes=scratch,
        compiler_params=pltpu.CompilerParams(
            collective_id=0, has_side_effects=True, vmem_limit_bytes=40 * 2**20
        ),
    )(coarse_in, out_grad, up_weight, conv_weight)
    return pl.pallas_call(
        functools.partial(last_kernel, 1.0 / math.sqrt(every_cell)),
        name="scale_outputs",
        out_shape=(
            jax.ShapeDtypeStruct((4, 8, 512), BF16),
            jax.ShapeDtypeStruct((64, C, C), F32),
            jax.ShapeDtypeStruct((27, C, C), F32),
        ),
        in_specs=[whole] * 3,
        out_specs=(whole, whole, whole),
        compiler_params=pltpu.CompilerParams(vmem_limit_bytes=32 * 2**20),
    )(coarse, fin_up, fin_conv)


def solution(mesh):
    sizes = tuple(mesh.shape[a] for a in ("gx", "gy", "gz"))
    in_specs = (P("gx", "gy", "gz"), P("gx", "gy", "gz"), P(), P())
    out_specs = (P("gx", "gy", "gz"), P(), P())
    return jax.shard_map(
        functools.partial(local, sizes), mesh=mesh, in_specs=in_specs, out_specs=out_specs, check_vma=False
    )
```

```python
import functools
import itertools
import math

import jax
import jax.numpy as jnp
from jax import lax
from jax.experimental import pallas as pl
from jax.experimental.pallas import tpu as pltpu
from jax.sharding import PartitionSpec as P

MESH = pl.DeviceIdType.MESH
F32 = jnp.float32
BF16 = jnp.bfloat16
C = 64
gelu_coef = 0.7978845608
gelu_cube = 0.044715
taps_by_parity = (((0, 3), (1, 1)), ((1, 2), (2, 0)))
NEIGHBOURS = sorted((o for o in itertools.product((-1, 0, 1), repeat=3) if any(o)), key=lambda o: -sum(map(abs, o)) - 9 * abs(o[0]))
G_PLANES = [0, 3, 4, 5, 6, 7, 8, 9, 12, 15]
U_PLANES = [1, 2, 10, 11, 13, 14]


def nt(left, right):
    return lax.dot_general(left, right, (((1,), (1,)), ((), ())), preferred_element_type=F32)


def nn(left, right):
    return jnp.dot(left, right, preferred_element_type=F32)


class Place:
    def __init__(self, sizes):
        self.sizes = sizes
        self.gx, self.gy, self.gz = (lax.axis_index(a) for a in ("gx", "gy", "gz"))
        self.nz, self.nx, self.ny = sizes[0] // 2, sizes[1], sizes[2]
        self.low = sizes[2] // 2
        self.z, self.x = self.gx // 2, self.gy
        self.y = self.gx % 2 * self.low + self.gz // 2
        self.core = self.gz % 2
        self.index = self.z * self.nx + self.x
        self.group = self.nz * self.nx
        self.row_group = 2 * self.low

    def neighbour(self, o):
        me = (self.gx, self.gy, self.gz)
        return tuple(lax.rem(m + d + n, n) for m, d, n in zip(me, o, self.sizes))

    def sibling(self):
        return (self.gx, self.gy, self.gz + 1 - 2 * self.core)

    def in_group(self, dz, dx):
        z, x = lax.rem(self.z + dz, self.nz), lax.rem(self.x + dx, self.nx)
        return (z * 2 + self.gx % 2, x, self.gz), z * self.nx + x

    def in_row(self, dy):
        y = lax.rem(self.y + dy, self.row_group)
        return (self.z * 2 + y // self.low, self.x, y % self.low * 2 + self.core)

    def group_steps(self):
        far = lambda o: -min(o[0], self.nz - o[0]) - min(o[1], self.nx - o[1])
        return sorted((o for o in itertools.product(range(self.nz), range(self.nx)) if any(o)), key=far)


def remote(src, dst, send, recv, device):
    return pltpu.make_async_remote_copy(
        src_ref=src, dst_ref=dst, send_sem=send, recv_sem=recv, device_id=device, device_id_type=MESH
    )


def halo(place, xt, edge, faces, extra, ys, yt, ct, ctr, send, recv):
    copies = {}
    planes, lanes = xt.shape[0], xt.shape[2] - 256
    inner = planes - 2 * edge
    for i, (ox, oy, oz) in enumerate(NEIGHBOURS):
        device = place.neighbour((ox, oy, oz))
        zs, zd = {
            0: (pl.ds(0, lanes), pl.ds(128, lanes)),
            1: (pl.ds(lanes - 128, 128), pl.ds(0, 128)),
            -1: (pl.ds(0, 128), pl.ds(lanes + 128, 128)),
        }[oz]
        side, end = (1 - oy) // 2, (1 - ox) // 2
        if oy == 0:
            zs = pl.ds(zs.start + 128, zs.size)
            if ox == 0:
                xs, xd = pl.ds(edge, inner), pl.ds(edge, inner)
            elif oz == 0:
                xs, xd = faces[end]
            else:
                xs, xd = (
                    (pl.ds(inner, edge), pl.ds(0, edge)),
                    (pl.ds(edge, edge), pl.ds(planes - edge, edge)),
                )[end]
            src, dst = xt.at[xs, :, zs], xt.at[xd, :, zd]
        elif ox == 0:
            src, dst = ys.at[side, :, zs], yt.at[side, :, zd]
        else:
            src, dst = ct.at[end, side], ctr.at[end, side, 1 - oz]
        copies[ox, oy, oz] = remote(src, dst, send.at[i], recv.at[i], device)
        if extra is not None and ox != 0 and (oy, oz) == (0, 0):
            source, target = extra
            copies[ox, None, None] = remote(
                source.at[end], target.at[end], send.at[26 + end], recv.at[26 + end], device
            )
    for copy in copies.values():
        copy.start()
    return copies


class AllReduce:
    def __init__(self, place, total, fin, r1, s, r2, r3, sems):
        self.place, self.total, self.fin = place, total, fin
        self.r1, self.s, self.r2, self.r3, self.sems = r1, s, r2, r3, sems
        self.half = total.shape[0] // 2
        self.piece = self.half // place.group
        self.used = 0
        self.flight, self.sent = [], []

    def send(self, src, dst, device):
        i = self.used
        self.used += 1
        copy = remote(src, dst, self.sems.at[0, i], self.sems.at[1, i], device)
        copy.start()
        self.flight.append(copy)

    def arrive(self):
        for copy in self.flight:
            copy.wait_recv()
        self.sent += self.flight
        self.flight = []

    def finish(self):
        self.arrive()
        self.store.wait()
        for copy in self.sent:
            copy.wait_send()

    def mine(self, index, size):
        return pl.ds(pl.multiple_of(index * size, size), size)

    def pair(self):
        p = self.place
        self.send(self.total.at[self.mine(1 - p.core, self.half)], self.r1, p.sibling())

    def scatter(self):
        p = self.place
        self.arrive()
        self.s[...] = (self.total[self.mine(p.core, self.half), :] + self.r1[...]).astype(BF16)
        for k, o in enumerate(p.group_steps()):
            device, index = p.in_group(*o)
            self.send(self.s.at[self.mine(index, self.piece)], self.r2.at[k], device)

    def exchange(self):
        p = self.place
        self.arrive()
        total = self.s[self.mine(p.index, self.piece), :].astype(F32)
        for k in range(p.group - 1):
            total = total + self.r2[k].astype(F32)
        self.r3[p.y] = total.astype(BF16)
        for dy in range(1, p.row_group):
            self.send(self.r3.at[p.y], self.r3.at[p.y], p.in_row(dy))

    def spot(self):
        p = self.place
        return pl.ds(pl.multiple_of(p.core * self.half + p.index * self.piece, self.piece), self.piece)

    def gather(self):
        p = self.place
        self.arrive()
        total = self.r3[0].astype(F32)
        for k in range(1, p.row_group):
            total = total + self.r3[k].astype(F32)
        self.fin[self.spot(), :] = total.astype(BF16)
        for o in p.group_steps():
            device, _ = p.in_group(*o)
            self.send(self.fin.at[self.spot()], self.fin.at[self.spot()], device)

    def share(self, out, sem):
        p = self.place
        self.arrive()
        spot = self.mine(p.core, self.half)
        self.send(self.fin.at[spot], out.at[spot], p.sibling())
        self.store = pltpu.make_async_copy(self.fin.at[spot], out.at[spot], sem)
        self.store.start()


def main_kernel(
    sizes, u_in, g_in, wu_in, wc_in,
    coarse_out, out_up, out_conv,
    ub, wu, wc, ue, ue1, uc, uce, xt, ysf, ys, yt, ct, ctr, ctf, yf, yr, ge, ga, gb,
    wp, cw, w3, uw, uwt, pre, slope, ht, gp,
    pxt, pys, pyt, pct, pctr, pyf, pyr, pe, co, gc,
    a_up, a_conv, fin_up, fin_conv, up_r1, up_s, up_r2, up_r3, cv_r1, cv_s, cv_r2, cv_r3,
    local_sems, g_sems, p_sems, up_sems, cv_sems,
):
    place = Place(sizes)
    barrier = pltpu.get_barrier_semaphore()
    partners = [place.neighbour(o) for o in NEIGHBOURS]
    partners += [place.in_group(*o)[0] for o in place.group_steps()]
    partners += [place.in_row(dy) for dy in range(1, place.row_group)]
    partners += [place.sibling()]
    for device in partners:
        pl.semaphore_signal(barrier, inc=1, device_id=device, device_id_type=MESH)
    loads = [
        pltpu.make_async_copy(u_in, ub, local_sems.at[0]),
        pltpu.make_async_copy(g_in.at[pl.ds(0, 7)], xt.at[pl.ds(3, 7), :, pl.ds(128, 1024)], local_sems.at[1]),
        pltpu.make_async_copy(wu_in, wu, local_sems.at[2]),
        pltpu.make_async_copy(wc_in, wc, local_sems.at[3]),
        pltpu.make_async_copy(g_in.at[7], xt.at[12, :, pl.ds(128, 1024)], local_sems.at[4]),
    ]
    for load in loads:
        load.start()

    zero_rows = jnp.zeros((4, 1024), F32)
    for side in range(2):
        ysf[side, 12:16, :] = zero_rows
    loads[0].wait()
    for x in range(4):
        rows = ub[x].astype(F32)
        ue[1 + x, 8:16, 128:640] = rows
        plane = U_PLANES[1 + x]
        for z, lane in ((0, 128), (384, 1024)):
            both = jnp.concatenate([rows[:, z : z + 128], rows[:, z : z + 128]], axis=0)
            xt[plane, :, lane : lane + 128] = both.astype(BF16)
        if x in (0, 3):
            uc[(3 - x) // 3] = jnp.concatenate([rows[:, 0:256], rows[:, 256:512]], axis=0).astype(BF16)
        for side, row in ((0, 7), (1, 0)):
            ysf[side, 8 + x : 9 + x, 0:256] = rows[row : row + 1, 0:256]
            ysf[side, 8 + x : 9 + x, 256:768] = jnp.zeros((1, 512), F32)
            ysf[side, 8 + x : 9 + x, 768:1024] = rows[row : row + 1, 256:512]
    loads[1].wait()
    loads[4].wait()
    for x in range(8):
        block = xt[G_PLANES[1 + x], :, 128:1152].astype(F32)
        ysf[0, x : x + 1, :] = block[15:16]
        ysf[1, x : x + 1, :] = block[0:1]
    for side in range(2):
        ys[side] = ysf[side].astype(BF16)
        for end, x, xc in ((0, 7, 3), (1, 0, 0)):
            ctf[end, side, 0, 8:16, :] = jnp.zeros((8, 128), F32)
            for j in range(8):
                ctf[end, side, 0, j : j + 1, :] = ysf[side, x : x + 1, 128 * j : 128 * j + 128]
            for j, lane in enumerate((0, 128, 768, 896)):
                ctf[end, side, 0, 8 + j : 9 + j, :] = ysf[side, 8 + xc : 9 + xc, lane : lane + 128]
            ct[end, side] = ctf[end, side, 0].astype(BF16)
    pl.semaphore_wait(barrier, len(partners))
    copies = halo(
        place, xt, 2, ((12, 0), (3, 15)), (uc, uce), ys, yt, ct, ctr, g_sems.at[0], g_sems.at[1]
    )

    loads[2].wait()
    loads[3].wait()
    blank = jnp.zeros((C, C), BF16)
    for q in range(16):
        k0, k1, k2, k3 = (wu[4 * q + k] for k in range(4))
        wp[q, 0:64, :] = jnp.concatenate([k3, blank], axis=1)
        wp[q, 64:128, :] = jnp.concatenate([k1, k2], axis=1)
        wp[q, 128:192, :] = jnp.concatenate([blank, k0], axis=1)
        wp[q, 192:256, :] = jnp.zeros((C, 2 * C), BF16)
        w3[q, :, 0:128] = jnp.concatenate([k0, k1], axis=1)
        w3[q, :, 128:256] = jnp.concatenate([k2, k3], axis=1)
    for dx in range(3):
        for dy in range(3):
            d0, d1, d2 = (wc[9 * dx + 3 * dy + d] for d in range(3))
            tap = jnp.concatenate(
                [
                    jnp.concatenate([d2, d1, d0, blank], axis=1),
                    jnp.concatenate([blank, d2, d1, d0], axis=1),
                ],
                axis=0,
            )
            for py in range(2):
                lane = 256 * (4 * dx + py - dy + 2)
                cw[128 * py : 128 * py + 128, lane : lane + 256] = tap
        cw[128:256, 1024 * dx : 1024 * dx + 256] = jnp.zeros((128, 256), BF16)
        cw[0:128, 1024 * dx + 768 : 1024 * dx + 1024] = jnp.zeros((128, 256), BF16)

    for copy in copies.values():
        copy.wait_recv()
    ctf[...] = ctr[...].astype(F32)
    for side in range(2):
        yf[side, 0:16, :] = yt[side].astype(F32)
        for end in range(2):
            for j in range(10):
                tile, row = (0, 7) if j == 0 else (2, 0) if j == 9 else (1, j - 1)
                yf[side, 16 + end : 17 + end, 128 * j : 128 * j + 128] = ctf[end, side, tile, row : row + 1, :]
            for j in range(6):
                tile, row = (0, 11) if j == 0 else (2, 8) if j == 5 else (1, 7 + j)
                ue[5 * end, 7 + 9 * side : 8 + 9 * side, 128 * j : 128 * j + 128] = ctf[
                    end, side, tile, row : row + 1, :
                ]
        for x in range(1, 5):
            row = slice(7 + x, 8 + x)
            ue[x, 7 + 9 * side : 8 + 9 * side, 0:384] = yf[side, row, 0:384]
            ue[x, 7 + 9 * side : 8 + 9 * side, 384:768] = yf[side, row, 896:1280]
    for end in range(2):
        face = uce[end].astype(F32)
        ue[5 * end, 8:16, 128:384] = face[0:8]
        ue[5 * end, 8:16, 384:640] = face[8:16]
    for x in range(6):
        ue[x, 8:16, 0:128] = xt[U_PLANES[x], :, 0:128].astype(F32)[0:8]
        ue[x, 8:16, 640:768] = xt[U_PLANES[x], :, 1152:1280].astype(F32)[0:8]
    for x in range(6):
        ue1[x] = pltpu.roll(ue[x], 768 - 64, 1)[:, :640]
    for sx in range(3):
        for sy in range(3):
            rows = []
            for zc in range(8):
                if zc % 2:
                    part = ue[sx : sx + 4, 7 + sy : 15 + sy, 64 * (zc + 1) : 64 * (zc + 1) + 256]
                else:
                    part = ue1[sx : sx + 4, 7 + sy : 15 + sy, 64 * zc : 64 * zc + 256]
                rows.append(part.reshape(32, 256))
            window = jnp.concatenate(rows, axis=0)
            uw[3 * sx + sy] = window.astype(BF16)
            uwt[3 * sx + sy] = window.T.astype(BF16)[:192]

    for px in range(2):
        for py in range(2):
            total = None
            for sx, kx in taps_by_parity[px]:
                for sy, ky in taps_by_parity[py]:
                    part = nn(uw[3 * sx + sy], wp[4 * kx + ky])
                    total = part if total is None else total + part
            total = total.reshape(8, 4, 8, 128)
            for xc in range(4):
                pre[:, 2 * xc + px, :, 128 * py : 128 * py + 128] = total[:, xc]
    for zc in range(0, 8, 2):
        v = pre[zc : zc + 2].reshape(128, 256)
        square = v * v
        tangent = jnp.tanh(gelu_coef * (v + gelu_cube * (square * v)))
        hidden = 0.5 * v * (1.0 + tangent)
        ht[:, 64 * zc : 64 * zc + 128] = hidden.T.astype(BF16)
        slope[64 * zc : 64 * zc + 128, :] = 0.5 * (1.0 + tangent) + 0.5 * v * (
            1.0 - tangent * tangent
        ) * gelu_coef * (1.0 + 3.0 * gelu_cube * square)

    turn = xt.shape[2] - 64
    for side in range(2):
        yr[side] = pltpu.roll(yf[side], turn, 1)[:, :1152]
    for x in range(10):
        turned = pltpu.roll(xt[G_PLANES[x]].astype(F32), turn, 1)
        row = 16 if x == 0 else 17 if x == 9 else x - 1
        for pair in range(9):
            lanes = slice(128 * pair, 128 * pair + 128)
            ge[pair, x, 8:24, :] = turned[:, lanes]
            ge[pair, x, 7:8, :] = yr[0, row : row + 1, lanes]
            ge[pair, x, 24:25, :] = yr[1, row : row + 1, lanes]
    for pair in range(9):
        for ky in range(4):
            rows = [ge[pair, x, pl.ds(7 + ky, 8, stride=2), :] for x in range(10)]
            ga[ky, pair] = jnp.concatenate(rows, axis=0).astype(BF16)
            gb[ky, pair] = jnp.concatenate(rows[1:9], axis=0).astype(BF16)

    def window(dx, ky):
        parts = []
        for zc in range(8):
            if dx == 1:
                pairs = [gb[ky, zc + s] for s in range(2)]
            else:
                first = 16 - 8 * dx
                pairs = [ga[ky, zc + s, first : first + 64] for s in range(2)]
            parts.append(jnp.concatenate(pairs, axis=1))
        return jnp.concatenate(parts, axis=0)

    total = None
    for dx in range(3):
        for ky in range(4):
            lane = 256 * (4 * dx + ky)
            part = nt(window(dx, ky), cw[:, lane : lane + 256])
            total = part if total is None else total + part
    gp[...] = (total * slope[...]).astype(BF16).astype(F32).reshape(8, 8, 8, 256)

    low = lax.broadcasted_iota(jnp.int32, (C, 2 * C), 1) < C
    for px in range(2):
        for py in range(2):
            rows = [gp[:, 2 * xc + px, :, 128 * py : 128 * py + 128] for xc in range(4)]
            grad = jnp.stack(rows, axis=1).reshape(256, 128).astype(BF16)
            for sx, kx in taps_by_parity[px]:
                for sy, ky in taps_by_parity[py]:
                    q = 4 * kx + ky
                    part = nn(uwt[3 * sx + sy], grad)
                    a_up[128 * q : 128 * q + 64, :] = part[64:128]
                    a_up[128 * q + 64 : 128 * q + 128, :] = jnp.where(low, part[0:64], part[128:192])
    up = AllReduce(place, a_up, fin_up, up_r1, up_s, up_r2, up_r3, up_sems)
    up.pair()

    for dx in range(3):
        products = [
            nn(ht[0:128, :], window(dx, 0)),
            nn(ht[...], window(dx, 1)),
            nn(ht[...], window(dx, 2)),
            nn(ht[128:256, :], window(dx, 3)),
        ]
        for dy in range(3):
            part = products[2 - dy][:128] + products[3 - dy][-128:]
            gc[3 * dx + dy] = part[:64] + pltpu.roll(part[64:], 256 - 64, 1)
    for t in range(9):
        a_conv[64 * t : 64 * t + 64, :] = gc[t, :, 0:128]
    for m in range(5):
        if m < 4:
            other = pltpu.roll(gc[2 * m + 1, :, 128:256], 64, 1)
            joined = jnp.where(low, gc[2 * m, :, 128:256], other)
        else:
            joined = gc[8, :, 128:256]
        a_conv[64 * (9 + m) : 64 * (10 + m), :] = joined
    a_conv[896:1024, :] = jnp.zeros((128, 128), F32)
    conv = AllReduce(place, a_conv, fin_conv, cv_r1, cv_s, cv_r2, cv_r3, cv_sems)
    conv.pair()
    up.scatter()
    conv.scatter()

    for x in range(8):
        for zc in range(8):
            block = gp[zc, x]
            rows = jnp.concatenate([block[:, 0:128], block[:, 128:256]], axis=0)
            pxt[1 + x, :, 128 * zc + 128 : 128 * zc + 256] = rows.astype(BF16)
            pys[0, x : x + 1, 128 * zc : 128 * zc + 128] = gp[zc, x, 7:8, 128:256]
            pys[1, x : x + 1, 128 * zc : 128 * zc + 128] = gp[zc, x, 0:1, 0:128]
            if x in (0, 7):
                pct[(7 - x) // 7, 0, zc : zc + 1, :] = gp[zc, x, 7:8, 128:256]
                pct[(7 - x) // 7, 1, zc : zc + 1, :] = gp[zc, x, 0:1, 0:128]
    p_copies = halo(
        place, pxt, 1, ((8, 0), (1, 9)), None, pys, pyt, pct, pctr, p_sems.at[0], p_sems.at[1]
    )
    up.exchange()
    conv.exchange()

    for copy in p_copies.values():
        copy.wait_recv()
    for side in range(2):
        pyf[side, 0:8, :] = pyt[side]
        for end in range(2):
            for j in range(10):
                tile, row = (0, 7) if j == 0 else (2, 0) if j == 9 else (1, j - 1)
                pyf[side, 8 + end : 9 + end, 128 * j : 128 * j + 128] = pctr[end, side, tile, row : row + 1, :]
        pyr[side] = pltpu.roll(pyf[side], turn, 1)[:, :1152]
    for x in range(10):
        turned = pltpu.roll(pxt[x].astype(F32), turn, 1)
        row = 8 if x == 0 else 9 if x == 9 else x - 1
        for pair in range(9):
            lanes = slice(128 * pair, 128 * pair + 128)
            pe[pair, x, 0, 8:16, :] = turned[0:8, lanes]
            pe[pair, x, 1, 8:16, :] = turned[8:16, lanes]
            pe[pair, x, 0, 16:17, :] = pyr[1, row : row + 1, lanes]
            pe[pair, x, 1, 7:8, :] = pyr[0, row : row + 1, lanes]
    total = None
    for kx in range(4):
        for ky in range(4):
            parity, first = ((1, 7), (0, 8), (1, 8), (0, 9))[ky]
            pairs = [
                jnp.concatenate([pe[pair, 2 * xc + kx, parity, first : first + 8, :] for xc in range(4)], axis=0)
                for pair in range(9)
            ]
            rows = [jnp.concatenate([pairs[zc], pairs[zc + 1]], axis=1) for zc in range(8)]
            part = nt(jnp.concatenate(rows, axis=0).astype(BF16), w3[4 * kx + ky])
            total = part if total is None else total + part
        if kx == 1:
            up.gather()
    conv.gather()
    total = total.reshape(8, 4, 8, C)
    for zc in range(0, 8, 2):
        co[:, :, 64 * zc : 64 * zc + 128] = jnp.concatenate([total[zc], total[zc + 1]], axis=2).astype(BF16)
    store = pltpu.make_async_copy(co, coarse_out, local_sems.at[5])
    store.start()
    up.share(out_up, local_sems.at[6])
    conv.share(out_conv, local_sems.at[7])
    up.finish()
    conv.finish()
    store.wait()
    for copy in [*copies.values(), *p_copies.values()]:
        copy.wait_send()


def last_kernel(
    factor, coarse, in_up, in_conv, coarse_out, up_out, conv_out, fin_up, fin_conv, up, conv, in_sems, out_sems
):
    through = pltpu.make_async_copy(coarse, coarse_out, out_sems.at[5])
    through.start()
    parts = [pl.ds(512 * i, 512) for i in range(4)]
    loads = [pltpu.make_async_copy(in_up.at[p], fin_up.at[p], in_sems.at[i]) for i, p in enumerate(parts)]
    loads.append(pltpu.make_async_copy(in_conv, fin_conv, in_sems.at[4]))
    for load in loads:
        load.start()
    stores = []
    for i in range(4):
        loads[i].wait()
        for q in range(4 * i, 4 * i + 4):
            first = fin_up[128 * q : 128 * q + 64, :].astype(F32) * factor
            second = fin_up[128 * q + 64 : 128 * q + 128, :].astype(F32) * factor
            up[4 * q + 1] = first[:, :C]
            up[4 * q + 2] = first[:, C:]
            up[4 * q + 3] = second[:, :C]
            up[4 * q] = second[:, C:]
        part = pl.ds(16 * i, 16)
        stores.append(pltpu.make_async_copy(up.at[part], up_out.at[part], out_sems.at[i]))
        stores[-1].start()
    loads[4].wait()
    for t in range(9):
        both = fin_conv[64 * t : 64 * t + 64, :].astype(F32) * factor
        conv[3 * t + 2] = both[:, :C]
        conv[3 * t + 1] = both[:, C:]
        m = t // 2
        rest = fin_conv[64 * (9 + m) : 64 * (10 + m), :].astype(F32) * factor
        conv[3 * t] = rest[:, C:] if t % 2 else rest[:, :C]
    stores.append(pltpu.make_async_copy(conv, conv_out, out_sems.at[4]))
    stores[-1].start()
    for store in stores:
        store.wait()
    through.wait()


def local(sizes, coarse_in, out_grad, up_weight, conv_weight):
    every_cell = 2048 * sizes[0] * sizes[1] * sizes[2]
    group = sizes[0] // 2 * sizes[1]
    row_group = sizes[2] // 2 * 2
    up_piece, cv_piece = 1024 // group, 512 // group
    messages = 2 + 2 * (group - 1) + row_group - 1
    vmem = pltpu.VMEM
    dma = pltpu.SemaphoreType.DMA
    anywhere = pl.BlockSpec(memory_space=pl.ANY)
    scratch = [
        vmem((4, 8, 512), BF16), vmem((64, C, C), BF16), vmem((27, C, C), BF16),
        vmem((6, 24, 768), F32), vmem((6, 24, 640), F32), vmem((2, 16, 256), BF16), vmem((2, 16, 256), BF16),
        vmem((16, 16, 1280), BF16), vmem((2, 16, 1024), F32), vmem((2, 16, 1024), BF16),
        vmem((2, 16, 1280), BF16), vmem((2, 2, 16, 128), BF16), vmem((2, 2, 3, 16, 128), BF16),
        vmem((2, 2, 3, 16, 128), F32), vmem((2, 24, 1280), F32), vmem((2, 24, 1152), F32),
        vmem((9, 10, 32, 128), F32), vmem((4, 9, 80, 128), BF16), vmem((4, 9, 64, 128), BF16),
        vmem((16, 256, 128), BF16), vmem((256, 3072), BF16), vmem((16, 64, 256), BF16),
        vmem((9, 256, 256), BF16), vmem((9, 192, 256), BF16),
        vmem((8, 8, 8, 256), F32), vmem((512, 256), F32), vmem((256, 512), BF16), vmem((8, 8, 8, 256), F32),
        vmem((10, 16, 1280), BF16), vmem((2, 8, 1024), F32), vmem((2, 8, 1280), F32),
        vmem((2, 2, 8, 128), F32), vmem((2, 2, 3, 8, 128), F32), vmem((2, 16, 1280), F32),
        vmem((2, 16, 1152), F32), vmem((9, 10, 2, 24, 128), F32), vmem((4, 8, 512), BF16),
        vmem((9, 64, 256), F32),
        vmem((2048, 128), F32), vmem((1024, 128), F32), vmem((2048, 128), BF16), vmem((1024, 128), BF16),
        vmem((1024, 128), F32), vmem((1024, 128), BF16), vmem((group - 1, up_piece, 128), BF16),
        vmem((row_group, up_piece, 128), BF16),
        vmem((512, 128), F32), vmem((512, 128), BF16), vmem((group - 1, cv_piece, 128), BF16),
        vmem((row_group, cv_piece, 128), BF16),
        dma((8,)), dma((2, 28)), dma((2, 26)), dma((2, messages)), dma((2, messages)),
    ]
    coarse, fin_up, fin_conv = pl.pallas_call(
        functools.partial(main_kernel, sizes),
        name="halo_compute_reduce",
        out_shape=(
            jax.ShapeDtypeStruct((4, 8, 512), BF16),
            jax.ShapeDtypeStruct((2048, 128), BF16),
            jax.ShapeDtypeStruct((1024, 128), BF16),
        ),
        in_specs=[anywhere] * 4,
        out_specs=(anywhere,) * 3,
        scratch_shapes=scratch,
        compiler_params=pltpu.CompilerParams(
            collective_id=0, has_side_effects=True, vmem_limit_bytes=60 * 2**20
        ),
    )(coarse_in, out_grad, up_weight, conv_weight)
    return pl.pallas_call(
        functools.partial(last_kernel, 1.0 / math.sqrt(every_cell)),
        name="scale_outputs",
        out_shape=(
            jax.ShapeDtypeStruct((4, 8, 512), BF16),
            jax.ShapeDtypeStruct((64, C, C), F32),
            jax.ShapeDtypeStruct((27, C, C), F32),
        ),
        in_specs=[anywhere] * 3,
        out_specs=(anywhere,) * 3,
        scratch_shapes=[
            vmem((2048, 128), BF16), vmem((1024, 128), BF16), vmem((64, C, C), F32), vmem((27, C, C), F32),
            dma((5,)), dma((6,)),
        ],
        compiler_params=pltpu.CompilerParams(vmem_limit_bytes=60 * 2**20),
    )(coarse, fin_up, fin_conv)


def solution(mesh):
    sizes = tuple(mesh.shape[a] for a in ("gx", "gy", "gz"))
    in_specs = (P("gx", "gy", "gz"), P("gx", "gy", "gz"), P(), P())
    out_specs = (P("gx", "gy", "gz"), P(), P())
    return jax.shard_map(
        functools.partial(local, sizes), mesh=mesh, in_specs=in_specs, out_specs=out_specs, check_vma=False
    )
```

```python
import functools
import itertools
import math

import jax
import jax.numpy as jnp
from jax import lax
from jax.experimental import pallas as pl
from jax.experimental.pallas import tpu as pltpu
from jax.sharding import PartitionSpec as P

MESH = pl.DeviceIdType.MESH
F32 = jnp.float32
BF16 = jnp.bfloat16
C = 64
gelu_coef = 0.7978845608
gelu_cube = 0.044715
taps_by_parity = (((0, 3), (1, 1)), ((1, 2), (2, 0)))
NEIGHBOURS = sorted((o for o in itertools.product((-1, 0, 1), repeat=3) if any(o)), key=lambda o: (-abs(o[0]), sum(map(abs, o))))
G_PLANES = [0, 3, 4, 5, 6, 7, 8, 9, 12, 15]
U_PLANES = [1, 2, 10, 11, 13, 14]


def nt(left, right):
    return lax.dot_general(left, right, (((1,), (1,)), ((), ())), preferred_element_type=F32)


def nn(left, right):
    return jnp.dot(left, right, preferred_element_type=F32)


class Place:
    def __init__(self, sizes):
        self.sizes = sizes
        self.gx, self.gy, self.gz = (lax.axis_index(a) for a in ("gx", "gy", "gz"))
        self.nz, self.nx, self.ny = sizes[0] // 2, sizes[1], sizes[2]
        self.low = sizes[2] // 2
        self.z, self.x = self.gx // 2, self.gy
        self.y = self.gx % 2 * self.low + self.gz // 2
        self.core = self.gz % 2
        self.index = self.z * self.nx + self.x
        self.group = self.nz * self.nx
        self.row_group = 2 * self.low

    def neighbour(self, o):
        me = (self.gx, self.gy, self.gz)
        return tuple(lax.rem(m + d + n, n) for m, d, n in zip(me, o, self.sizes))

    def sibling(self):
        return (self.gx, self.gy, self.gz + 1 - 2 * self.core)

    def in_group(self, dz, dx):
        z, x = lax.rem(self.z + dz, self.nz), lax.rem(self.x + dx, self.nx)
        return (z * 2 + self.gx % 2, x, self.gz), z * self.nx + x

    def in_row(self, dy):
        y = lax.rem(self.y + dy, self.row_group)
        return (self.z * 2 + y // self.low, self.x, y % self.low * 2 + self.core)

    def group_steps(self):
        far = lambda o: -min(o[0], self.nz - o[0]) - min(o[1], self.nx - o[1])
        return sorted((o for o in itertools.product(range(self.nz), range(self.nx)) if any(o)), key=far)


def remote(src, dst, send, recv, device):
    return pltpu.make_async_remote_copy(
        src_ref=src, dst_ref=dst, send_sem=send, recv_sem=recv, device_id=device, device_id_type=MESH
    )


def halo(place, xt, edge, faces, extra, ys, yt, ct, ctr, send, recv):
    copies = {}
    planes, lanes = xt.shape[0], xt.shape[2] - 256
    inner = planes - 2 * edge
    for i, (ox, oy, oz) in enumerate(NEIGHBOURS):
        device = place.neighbour((ox, oy, oz))
        zs, zd = {
            0: (pl.ds(0, lanes), pl.ds(128, lanes)),
            1: (pl.ds(lanes - 128, 128), pl.ds(0, 128)),
            -1: (pl.ds(0, 128), pl.ds(lanes + 128, 128)),
        }[oz]
        side, end = (1 - oy) // 2, (1 - ox) // 2
        if oy == 0:
            zs = pl.ds(zs.start + 128, zs.size)
            if ox == 0:
                xs, xd = pl.ds(edge, inner), pl.ds(edge, inner)
            elif oz == 0:
                xs, xd = faces[end]
            else:
                xs, xd = (
                    (pl.ds(inner, edge), pl.ds(0, edge)),
                    (pl.ds(edge, edge), pl.ds(planes - edge, edge)),
                )[end]
            src, dst = xt.at[xs, :, zs], xt.at[xd, :, zd]
        elif ox == 0:
            src, dst = ys.at[side, :, zs], yt.at[side, :, zd]
        else:
            src, dst = ct.at[end, side], ctr.at[end, side, 1 - oz]
        copies[ox, oy, oz] = remote(src, dst, send.at[i], recv.at[i], device)
        if extra is not None and ox != 0 and (oy, oz) == (0, 0):
            source, target = extra
            copies[ox, None, None] = remote(
                source.at[end], target.at[end], send.at[26 + end], recv.at[26 + end], device
            )
    for copy in copies.values():
        copy.start()
    return copies


class AllReduce:
    def __init__(self, place, total, fin, r1, s, r2, r3, sems):
        self.place, self.total, self.fin = place, total, fin
        self.r1, self.s, self.r2, self.r3, self.sems = r1, s, r2, r3, sems
        self.half = total.shape[0] // 2
        self.piece = self.half // place.group
        self.used = 0
        self.flight, self.sent = [], []

    def send(self, src, dst, device):
        i = self.used
        self.used += 1
        copy = remote(src, dst, self.sems.at[0, i], self.sems.at[1, i], device)
        copy.start()
        self.flight.append(copy)

    def arrive(self):
        for copy in self.flight:
            copy.wait_recv()
        self.sent += self.flight
        self.flight = []

    def finish(self):
        self.arrive()
        self.store.wait()
        for copy in self.sent:
            copy.wait_send()

    def mine(self, index, size):
        return pl.ds(pl.multiple_of(index * size, size), size)

    def pair(self, part=0, parts=1):
        p = self.place
        size = self.half // parts
        rows = pl.ds(pl.multiple_of((1 - p.core) * self.half + part * size, size), size)
        self.send(self.total.at[rows], self.r1.at[pl.ds(part * size, size)], p.sibling())

    def scatter(self):
        p = self.place
        self.arrive()
        self.s[...] = (self.total[self.mine(p.core, self.half), :] + self.r1[...]).astype(BF16)
        for k, o in enumerate(p.group_steps()):
            device, index = p.in_group(*o)
            self.send(self.s.at[self.mine(index, self.piece)], self.r2.at[k], device)

    def exchange(self):
        p = self.place
        self.arrive()
        total = self.s[self.mine(p.index, self.piece), :].astype(F32)
        for k in range(p.group - 1):
            total = total + self.r2[k].astype(F32)
        self.r3[p.y] = total.astype(BF16)
        for dy in range(1, p.row_group):
            self.send(self.r3.at[p.y], self.r3.at[p.y], p.in_row(dy))

    def spot(self):
        p = self.place
        return pl.ds(pl.multiple_of(p.core * self.half + p.index * self.piece, self.piece), self.piece)

    def gather(self):
        p = self.place
        self.arrive()
        total = self.r3[0].astype(F32)
        for k in range(1, p.row_group):
            total = total + self.r3[k].astype(F32)
        self.fin[self.spot(), :] = total.astype(BF16)
        for o in p.group_steps():
            device, _ = p.in_group(*o)
            self.send(self.fin.at[self.spot()], self.fin.at[self.spot()], device)

    def share(self, out, sem):
        p = self.place
        self.arrive()
        spot = self.mine(p.core, self.half)
        self.send(self.fin.at[spot], out.at[spot], p.sibling())
        self.store = pltpu.make_async_copy(self.fin.at[spot], out.at[spot], sem)
        self.store.start()


def main_kernel(
    sizes, u_in, g_in, wu_in, wc_in,
    coarse_out, out_up, out_conv,
    ub, wu, wc, ue, ue1, uc, uce, xt, ysf, ys, yt, ct, ctr, ctf, yf, yr, ge, ga, gb,
    wp, cw, w3, uw, uwt, pre, slope, ht, gp,
    pxt, pys, pyt, pct, pctr, pyf, pyr, pe, co, gc,
    a_up, a_conv, fin_up, fin_conv, up_r1, up_s, up_r2, up_r3, cv_r1, cv_s, cv_r2, cv_r3,
    local_sems, g_sems, p_sems, up_sems, cv_sems,
):
    place = Place(sizes)
    barrier = pltpu.get_barrier_semaphore()
    partners = [place.neighbour(o) for o in NEIGHBOURS]
    partners += [place.in_group(*o)[0] for o in place.group_steps()]
    partners += [place.in_row(dy) for dy in range(1, place.row_group)]
    partners += [place.sibling()]
    for device in partners:
        pl.semaphore_signal(barrier, inc=1, device_id=device, device_id_type=MESH)
    loads = [
        pltpu.make_async_copy(u_in, ub, local_sems.at[0]),
        pltpu.make_async_copy(g_in.at[pl.ds(0, 7)], xt.at[pl.ds(3, 7), :, pl.ds(128, 1024)], local_sems.at[1]),
        pltpu.make_async_copy(g_in.at[7], xt.at[12, :, pl.ds(128, 1024)], local_sems.at[2]),
        pltpu.make_async_copy(wu_in, wu, local_sems.at[3]),
        pltpu.make_async_copy(wc_in, wc, local_sems.at[4]),
    ]
    for load in loads:
        load.start()

    zero_rows = jnp.zeros((4, 1024), F32)
    for side in range(2):
        ysf[side, 12:16, :] = zero_rows
    loads[0].wait()
    for x in range(4):
        rows = ub[x].astype(F32)
        ue[1 + x, 8:16, 128:640] = rows
        plane = U_PLANES[1 + x]
        for z, lane in ((0, 128), (384, 1024)):
            both = jnp.concatenate([rows[:, z : z + 128], rows[:, z : z + 128]], axis=0)
            xt[plane, :, lane : lane + 128] = both.astype(BF16)
        if x in (0, 3):
            uc[(3 - x) // 3] = jnp.concatenate([rows[:, 0:256], rows[:, 256:512]], axis=0).astype(BF16)
        for side, row in ((0, 7), (1, 0)):
            ysf[side, 8 + x : 9 + x, 0:256] = rows[row : row + 1, 0:256]
            ysf[side, 8 + x : 9 + x, 256:768] = jnp.zeros((1, 512), F32)
            ysf[side, 8 + x : 9 + x, 768:1024] = rows[row : row + 1, 256:512]
    loads[1].wait()
    loads[2].wait()
    for x in range(8):
        block = xt[G_PLANES[1 + x], :, 128:1152].astype(F32)
        ysf[0, x : x + 1, :] = block[15:16]
        ysf[1, x : x + 1, :] = block[0:1]
    for side in range(2):
        ys[side] = ysf[side].astype(BF16)
        for end, x, xc in ((0, 7, 3), (1, 0, 0)):
            ctf[end, side, 0, 8:16, :] = jnp.zeros((8, 128), F32)
            for j in range(8):
                ctf[end, side, 0, j : j + 1, :] = ysf[side, x : x + 1, 128 * j : 128 * j + 128]
            for j, lane in enumerate((0, 128, 768, 896)):
                ctf[end, side, 0, 8 + j : 9 + j, :] = ysf[side, 8 + xc : 9 + xc, lane : lane + 128]
            ct[end, side] = ctf[end, side, 0].astype(BF16)
    pl.semaphore_wait(barrier, len(partners))
    copies = halo(
        place, xt, 2, ((12, 0), (3, 15)), (uc, uce), ys, yt, ct, ctr, g_sems.at[0], g_sems.at[1]
    )

    loads[3].wait()
    loads[4].wait()
    blank = jnp.zeros((C, C), BF16)
    for q in range(16):
        k0, k1, k2, k3 = (wu[4 * q + k] for k in range(4))
        wp[q, 0:64, :] = jnp.concatenate([k3, blank], axis=1)
        wp[q, 64:128, :] = jnp.concatenate([k1, k2], axis=1)
        wp[q, 128:192, :] = jnp.concatenate([blank, k0], axis=1)
        wp[q, 192:256, :] = jnp.zeros((C, 2 * C), BF16)
        w3[q, :, 0:128] = jnp.concatenate([k0, k1], axis=1)
        w3[q, :, 128:256] = jnp.concatenate([k2, k3], axis=1)
    for dx in range(3):
        for dy in range(3):
            d0, d1, d2 = (wc[9 * dx + 3 * dy + d] for d in range(3))
            tap = jnp.concatenate(
                [
                    jnp.concatenate([d2, d1, d0, blank], axis=1),
                    jnp.concatenate([blank, d2, d1, d0], axis=1),
                ],
                axis=0,
            )
            for py in range(2):
                lane = 256 * (4 * dx + py - dy + 2)
                cw[128 * py : 128 * py + 128, lane : lane + 256] = tap
        cw[128:256, 1024 * dx : 1024 * dx + 256] = jnp.zeros((128, 256), BF16)
        cw[0:128, 1024 * dx + 768 : 1024 * dx + 1024] = jnp.zeros((128, 256), BF16)

    for copy in copies.values():
        copy.wait_recv()
    ctf[...] = ctr[...].astype(F32)
    for side in range(2):
        yf[side, 0:16, :] = yt[side].astype(F32)
        for end in range(2):
            for j in range(10):
                tile, row = (0, 7) if j == 0 else (2, 0) if j == 9 else (1, j - 1)
                yf[side, 16 + end : 17 + end, 128 * j : 128 * j + 128] = ctf[end, side, tile, row : row + 1, :]
            for j in range(6):
                tile, row = (0, 11) if j == 0 else (2, 8) if j == 5 else (1, 7 + j)
                ue[5 * end, 7 + 9 * side : 8 + 9 * side, 128 * j : 128 * j + 128] = ctf[
                    end, side, tile, row : row + 1, :
                ]
        for x in range(1, 5):
            row = slice(7 + x, 8 + x)
            ue[x, 7 + 9 * side : 8 + 9 * side, 0:384] = yf[side, row, 0:384]
            ue[x, 7 + 9 * side : 8 + 9 * side, 384:768] = yf[side, row, 896:1280]
    for end in range(2):
        face = uce[end].astype(F32)
        ue[5 * end, 8:16, 128:384] = face[0:8]
        ue[5 * end, 8:16, 384:640] = face[8:16]
    for x in range(6):
        ue[x, 8:16, 0:128] = xt[U_PLANES[x], :, 0:128].astype(F32)[0:8]
        ue[x, 8:16, 640:768] = xt[U_PLANES[x], :, 1152:1280].astype(F32)[0:8]
    for x in range(6):
        ue1[x] = pltpu.roll(ue[x], 768 - 64, 1)[:, :640]
    for sx in range(3):
        for sy in range(3):
            rows = []
            for zc in range(8):
                if zc % 2:
                    part = ue[sx : sx + 4, 7 + sy : 15 + sy, 64 * (zc + 1) : 64 * (zc + 1) + 256]
                else:
                    part = ue1[sx : sx + 4, 7 + sy : 15 + sy, 64 * zc : 64 * zc + 256]
                rows.append(part.reshape(32, 256))
            window = jnp.concatenate(rows, axis=0)
            uw[3 * sx + sy] = window.astype(BF16)
            uwt[3 * sx + sy] = window.T.astype(BF16)[:192]

    for px in range(2):
        for py in range(2):
            total = None
            for sx, kx in taps_by_parity[px]:
                for sy, ky in taps_by_parity[py]:
                    part = nn(uw[3 * sx + sy], wp[4 * kx + ky])
                    total = part if total is None else total + part
            total = total.reshape(8, 4, 8, 128)
            for xc in range(4):
                pre[:, 2 * xc + px, :, 128 * py : 128 * py + 128] = total[:, xc]
    for zc in range(0, 8, 2):
        v = pre[zc : zc + 2].reshape(128, 256)
        square = v * v
        tangent = jnp.tanh(gelu_coef * (v + gelu_cube * (square * v)))
        hidden = 0.5 * v * (1.0 + tangent)
        ht[:, 64 * zc : 64 * zc + 128] = hidden.T.astype(BF16)
        slope[64 * zc : 64 * zc + 128, :] = 0.5 * (1.0 + tangent) + 0.5 * v * (
            1.0 - tangent * tangent
        ) * gelu_coef * (1.0 + 3.0 * gelu_cube * square)

    turn = xt.shape[2] - 64
    for side in range(2):
        yr[side] = pltpu.roll(yf[side], turn, 1)[:, :1152]
    for x in range(10):
        turned = pltpu.roll(xt[G_PLANES[x]].astype(F32), turn, 1)
        row = 16 if x == 0 else 17 if x == 9 else x - 1
        for pair in range(9):
            lanes = slice(128 * pair, 128 * pair + 128)
            ge[pair, x, 8:24, :] = turned[:, lanes]
            ge[pair, x, 7:8, :] = yr[0, row : row + 1, lanes]
            ge[pair, x, 24:25, :] = yr[1, row : row + 1, lanes]
    for pair in range(9):
        for ky in range(4):
            rows = [ge[pair, x, pl.ds(7 + ky, 8, stride=2), :] for x in range(10)]
            ga[ky, pair] = jnp.concatenate(rows, axis=0).astype(BF16)
            gb[ky, pair] = jnp.concatenate(rows[1:9], axis=0).astype(BF16)

    def window(dx, ky):
        parts = []
        for zc in range(8):
            if dx == 1:
                pairs = [gb[ky, zc + s] for s in range(2)]
            else:
                first = 16 - 8 * dx
                pairs = [ga[ky, zc + s, first : first + 64] for s in range(2)]
            parts.append(jnp.concatenate(pairs, axis=1))
        return jnp.concatenate(parts, axis=0)

    low = lax.broadcasted_iota(jnp.int32, (C, 2 * C), 1) < C
    for dx in range(3):
        products = [
            nn(ht[0:128, :], window(dx, 0)),
            nn(ht[...], window(dx, 1)),
            nn(ht[...], window(dx, 2)),
            nn(ht[128:256, :], window(dx, 3)),
        ]
        for dy in range(3):
            part = products[2 - dy][:128] + products[3 - dy][-128:]
            gc[3 * dx + dy] = part[:64] + pltpu.roll(part[64:], 256 - 64, 1)
    for t in range(9):
        a_conv[64 * t : 64 * t + 64, :] = gc[t, :, 0:128]
    for m in range(5):
        if m < 4:
            other = pltpu.roll(gc[2 * m + 1, :, 128:256], 64, 1)
            joined = jnp.where(low, gc[2 * m, :, 128:256], other)
        else:
            joined = gc[8, :, 128:256]
        a_conv[64 * (9 + m) : 64 * (10 + m), :] = joined
    a_conv[896:1024, :] = jnp.zeros((128, 128), F32)
    conv = AllReduce(place, a_conv, fin_conv, cv_r1, cv_s, cv_r2, cv_r3, cv_sems)
    conv.pair()

    total = None
    for dx in range(3):
        for ky in range(4):
            lane = 256 * (4 * dx + ky)
            part = nt(window(dx, ky), cw[:, lane : lane + 256])
            total = part if total is None else total + part
    gp[...] = (total * slope[...]).astype(BF16).astype(F32).reshape(8, 8, 8, 256)

    conv.scatter()

    up = AllReduce(place, a_up, fin_up, up_r1, up_s, up_r2, up_r3, up_sems)
    for parities, (px, py) in enumerate(itertools.product(range(2), repeat=2)):
        rows = [gp[:, 2 * xc + px, :, 128 * py : 128 * py + 128] for xc in range(4)]
        grad = jnp.stack(rows, axis=1).reshape(256, 128).astype(BF16)
        for i, (sx, kx) in enumerate(taps_by_parity[px]):
            for j, (sy, ky) in enumerate(taps_by_parity[py]):
                row = 1024 * i + 256 * parities + 128 * j
                part = nn(uwt[3 * sx + sy], grad)
                a_up[row : row + 64, :] = part[64:128]
                a_up[row + 64 : row + 128, :] = jnp.where(low, part[0:64], part[128:192])
        up.pair(parities, 4)

    for x in range(8):
        for zc in range(8):
            block = gp[zc, x]
            rows = jnp.concatenate([block[:, 0:128], block[:, 128:256]], axis=0)
            pxt[1 + x, :, 128 * zc + 128 : 128 * zc + 256] = rows.astype(BF16)
            pys[0, x : x + 1, 128 * zc : 128 * zc + 128] = gp[zc, x, 7:8, 128:256]
            pys[1, x : x + 1, 128 * zc : 128 * zc + 128] = gp[zc, x, 0:1, 0:128]
            if x in (0, 7):
                pct[(7 - x) // 7, 0, zc : zc + 1, :] = gp[zc, x, 7:8, 128:256]
                pct[(7 - x) // 7, 1, zc : zc + 1, :] = gp[zc, x, 0:1, 0:128]
    up.scatter()
    conv.exchange()
    p_copies = halo(
        place, pxt, 1, ((8, 0), (1, 9)), None, pys, pyt, pct, pctr, p_sems.at[0], p_sems.at[1]
    )
    up.exchange()
    conv.gather()
    up.gather()

    for copy in p_copies.values():
        copy.wait_recv()
    for side in range(2):
        pyf[side, 0:8, :] = pyt[side]
        for end in range(2):
            for j in range(10):
                tile, row = (0, 7) if j == 0 else (2, 0) if j == 9 else (1, j - 1)
                pyf[side, 8 + end : 9 + end, 128 * j : 128 * j + 128] = pctr[end, side, tile, row : row + 1, :]
        pyr[side] = pltpu.roll(pyf[side], turn, 1)[:, :1152]
    for x in range(10):
        turned = pltpu.roll(pxt[x].astype(F32), turn, 1)
        row = 8 if x == 0 else 9 if x == 9 else x - 1
        for pair in range(9):
            lanes = slice(128 * pair, 128 * pair + 128)
            pe[pair, x, 0, 8:16, :] = turned[0:8, lanes]
            pe[pair, x, 1, 8:16, :] = turned[8:16, lanes]
            pe[pair, x, 0, 16:17, :] = pyr[1, row : row + 1, lanes]
            pe[pair, x, 1, 7:8, :] = pyr[0, row : row + 1, lanes]
    total = None
    for kx in range(4):
        for ky in range(4):
            parity, first = ((1, 7), (0, 8), (1, 8), (0, 9))[ky]
            pairs = [
                jnp.concatenate([pe[pair, 2 * xc + kx, parity, first : first + 8, :] for xc in range(4)], axis=0)
                for pair in range(9)
            ]
            rows = [jnp.concatenate([pairs[zc], pairs[zc + 1]], axis=1) for zc in range(8)]
            part = nt(jnp.concatenate(rows, axis=0).astype(BF16), w3[4 * kx + ky])
            total = part if total is None else total + part
    total = total.reshape(8, 4, 8, C)
    for zc in range(0, 8, 2):
        co[:, :, 64 * zc : 64 * zc + 128] = jnp.concatenate([total[zc], total[zc + 1]], axis=2).astype(BF16)
    store = pltpu.make_async_copy(co, coarse_out, local_sems.at[5])
    store.start()
    conv.share(out_conv, local_sems.at[6])
    up.share(out_up, local_sems.at[7])
    up.finish()
    conv.finish()
    store.wait()
    for copy in [*copies.values(), *p_copies.values()]:
        copy.wait_send()


def last_kernel(
    factor, coarse, in_up, in_conv, coarse_out, up_out, conv_out, fin_up, fin_conv, up, conv, in_sems, out_sems
):
    through = pltpu.make_async_copy(coarse, coarse_out, out_sems.at[5])
    through.start()
    parts = [pl.ds(512 * i, 512) for i in range(4)]
    loads = [pltpu.make_async_copy(in_up.at[p], fin_up.at[p], in_sems.at[i]) for i, p in enumerate(parts)]
    loads.append(pltpu.make_async_copy(in_conv, fin_conv, in_sems.at[4]))
    for load in loads:
        load.start()
    stores = []
    for i in range(4):
        loads[i].wait()
        for s in range(4 * i, 4 * i + 4):
            half, px, py, j = s // 8, s // 4 % 2, s // 2 % 2, s % 2
            q = 4 * taps_by_parity[px][half][1] + taps_by_parity[py][j][1]
            first = fin_up[128 * s : 128 * s + 64, :].astype(F32) * factor
            second = fin_up[128 * s + 64 : 128 * s + 128, :].astype(F32) * factor
            up[4 * q + 1] = first[:, :C]
            up[4 * q + 2] = first[:, C:]
            up[4 * q + 3] = second[:, :C]
            up[4 * q] = second[:, C:]
        kx = taps_by_parity[i % 2][i // 2][1]
        part = pl.ds(16 * kx, 16)
        stores.append(pltpu.make_async_copy(up.at[part], up_out.at[part], out_sems.at[i]))
        stores[-1].start()
    loads[4].wait()
    for t in range(9):
        both = fin_conv[64 * t : 64 * t + 64, :].astype(F32) * factor
        conv[3 * t + 2] = both[:, :C]
        conv[3 * t + 1] = both[:, C:]
        m = t // 2
        rest = fin_conv[64 * (9 + m) : 64 * (10 + m), :].astype(F32) * factor
        conv[3 * t] = rest[:, C:] if t % 2 else rest[:, :C]
    stores.append(pltpu.make_async_copy(conv, conv_out, out_sems.at[4]))
    stores[-1].start()
    for store in stores:
        store.wait()
    through.wait()


def local(sizes, coarse_in, out_grad, up_weight, conv_weight):
    every_cell = 2048 * sizes[0] * sizes[1] * sizes[2]
    group = sizes[0] // 2 * sizes[1]
    row_group = sizes[2] // 2 * 2
    up_piece, cv_piece = 1024 // group, 512 // group
    messages = 5 + 2 * (group - 1) + row_group - 1
    vmem = pltpu.VMEM
    dma = pltpu.SemaphoreType.DMA
    anywhere = pl.BlockSpec(memory_space=pl.ANY)
    scratch = [
        vmem((4, 8, 512), BF16), vmem((64, C, C), BF16), vmem((27, C, C), BF16),
        vmem((6, 24, 768), F32), vmem((6, 24, 640), F32), vmem((2, 16, 256), BF16), vmem((2, 16, 256), BF16),
        vmem((16, 16, 1280), BF16), vmem((2, 16, 1024), F32), vmem((2, 16, 1024), BF16),
        vmem((2, 16, 1280), BF16), vmem((2, 2, 16, 128), BF16), vmem((2, 2, 3, 16, 128), BF16),
        vmem((2, 2, 3, 16, 128), F32), vmem((2, 24, 1280), F32), vmem((2, 24, 1152), F32),
        vmem((9, 10, 32, 128), F32), vmem((4, 9, 80, 128), BF16), vmem((4, 9, 64, 128), BF16),
        vmem((16, 256, 128), BF16), vmem((256, 3072), BF16), vmem((16, 64, 256), BF16),
        vmem((9, 256, 256), BF16), vmem((9, 192, 256), BF16),
        vmem((8, 8, 8, 256), F32), vmem((512, 256), F32), vmem((256, 512), BF16), vmem((8, 8, 8, 256), F32),
        vmem((10, 16, 1280), BF16), vmem((2, 8, 1024), F32), vmem((2, 8, 1280), F32),
        vmem((2, 2, 8, 128), F32), vmem((2, 2, 3, 8, 128), F32), vmem((2, 16, 1280), F32),
        vmem((2, 16, 1152), F32), vmem((9, 10, 2, 24, 128), F32), vmem((4, 8, 512), BF16),
        vmem((9, 64, 256), F32),
        vmem((2048, 128), F32), vmem((1024, 128), F32), vmem((2048, 128), BF16), vmem((1024, 128), BF16),
        vmem((1024, 128), F32), vmem((1024, 128), BF16), vmem((group - 1, up_piece, 128), BF16),
        vmem((row_group, up_piece, 128), BF16),
        vmem((512, 128), F32), vmem((512, 128), BF16), vmem((group - 1, cv_piece, 128), BF16),
        vmem((row_group, cv_piece, 128), BF16),
        dma((8,)), dma((2, 28)), dma((2, 26)), dma((2, messages)), dma((2, messages)),
    ]
    coarse, fin_up, fin_conv = pl.pallas_call(
        functools.partial(main_kernel, sizes),
        name="halo_compute_reduce",
        out_shape=(
            jax.ShapeDtypeStruct((4, 8, 512), BF16),
            jax.ShapeDtypeStruct((2048, 128), BF16),
            jax.ShapeDtypeStruct((1024, 128), BF16),
        ),
        in_specs=[anywhere] * 4,
        out_specs=(anywhere,) * 3,
        scratch_shapes=scratch,
        compiler_params=pltpu.CompilerParams(
            collective_id=0, has_side_effects=True, vmem_limit_bytes=60 * 2**20
        ),
    )(coarse_in, out_grad, up_weight, conv_weight)
    return pl.pallas_call(
        functools.partial(last_kernel, 1.0 / math.sqrt(every_cell)),
        name="scale_outputs",
        out_shape=(
            jax.ShapeDtypeStruct((4, 8, 512), BF16),
            jax.ShapeDtypeStruct((64, C, C), F32),
            jax.ShapeDtypeStruct((27, C, C), F32),
        ),
        in_specs=[anywhere] * 3,
        out_specs=(anywhere,) * 3,
        scratch_shapes=[
            vmem((2048, 128), BF16), vmem((1024, 128), BF16), vmem((64, C, C), F32), vmem((27, C, C), F32),
            dma((5,)), dma((6,)),
        ],
        compiler_params=pltpu.CompilerParams(vmem_limit_bytes=60 * 2**20),
    )(coarse, fin_up, fin_conv)


def solution(mesh):
    sizes = tuple(mesh.shape[a] for a in ("gx", "gy", "gz"))
    in_specs = (P("gx", "gy", "gz"), P("gx", "gy", "gz"), P(), P())
    out_specs = (P("gx", "gy", "gz"), P(), P())
    return jax.shard_map(
        functools.partial(local, sizes), mesh=mesh, in_specs=in_specs, out_specs=out_specs, check_vma=False
    )
```

```python
import functools
import itertools
import math

import jax
import jax.numpy as jnp
from jax import lax
from jax.experimental import pallas as pl
from jax.experimental.pallas import tpu as pltpu
from jax.sharding import PartitionSpec as P

MESH = pl.DeviceIdType.MESH
F32 = jnp.float32
BF16 = jnp.bfloat16
C = 64
gelu_coef = 0.7978845608
gelu_cube = 0.044715
taps_by_parity = (((0, 3), (1, 1)), ((1, 2), (2, 0)))
NEIGHBOURS = sorted((o for o in itertools.product((-1, 0, 1), repeat=3) if any(o)), key=lambda o: (-abs(o[0]), sum(map(abs, o))))
G_PLANES = [0, 3, 4, 5, 6, 7, 8, 9, 12, 15]
U_PLANES = [1, 2, 10, 11, 13, 14]


def nt(left, right):
    return lax.dot_general(left, right, (((1,), (1,)), ((), ())), preferred_element_type=F32)


def nn(left, right):
    return jnp.dot(left, right, preferred_element_type=F32)


class Place:
    def __init__(self, sizes):
        self.sizes = sizes
        self.gx, self.gy, self.gz = (lax.axis_index(a) for a in ("gx", "gy", "gz"))
        self.nz, self.nx, self.ny = sizes[0] // 2, sizes[1], sizes[2]
        self.low = sizes[2] // 2
        self.z, self.x = self.gx // 2, self.gy
        self.y = self.gx % 2 * self.low + self.gz // 2
        self.core = self.gz % 2
        self.index = self.z * self.nx + self.x
        self.group = self.nz * self.nx
        self.row_group = 2 * self.low

    def neighbour(self, o):
        me = (self.gx, self.gy, self.gz)
        return tuple(lax.rem(m + d + n, n) for m, d, n in zip(me, o, self.sizes))

    def sibling(self):
        return (self.gx, self.gy, self.gz + 1 - 2 * self.core)

    def in_group(self, dz, dx):
        z, x = lax.rem(self.z + dz, self.nz), lax.rem(self.x + dx, self.nx)
        return (z * 2 + self.gx % 2, x, self.gz), z * self.nx + x

    def in_row(self, dy):
        y = lax.rem(self.y + dy, self.row_group)
        return (self.z * 2 + y // self.low, self.x, y % self.low * 2 + self.core)

    def group_steps(self):
        far = lambda o: -min(o[0], self.nz - o[0]) - min(o[1], self.nx - o[1])
        return sorted((o for o in itertools.product(range(self.nz), range(self.nx)) if any(o)), key=far)


def remote(src, dst, send, recv, device):
    return pltpu.make_async_remote_copy(
        src_ref=src, dst_ref=dst, send_sem=send, recv_sem=recv, device_id=device, device_id_type=MESH
    )


def await_bytes(ref, sem):
    pltpu.make_async_copy(ref, ref, sem).wait()


def halo(place, xt, edge, faces, extra, ys, yt, ct, ctr, sems):
    copies = []
    planes, lanes = xt.shape[0], xt.shape[2] - 256
    inner = planes - 2 * edge
    for ox, oy, oz in NEIGHBOURS:
        device = place.neighbour((ox, oy, oz))
        zs, zd = {
            0: (pl.ds(0, lanes), pl.ds(128, lanes)),
            1: (pl.ds(lanes - 128, 128), pl.ds(0, 128)),
            -1: (pl.ds(0, 128), pl.ds(lanes + 128, 128)),
        }[oz]
        side, end = (1 - oy) // 2, (1 - ox) // 2
        if oy == 0:
            zs = pl.ds(zs.start + 128, zs.size)
            if ox == 0:
                xs, xd = pl.ds(edge, inner), pl.ds(edge, inner)
            elif oz == 0:
                xs, xd = faces[end]
            else:
                xs, xd = (
                    (pl.ds(inner, edge), pl.ds(0, edge)),
                    (pl.ds(edge, edge), pl.ds(planes - edge, edge)),
                )[end]
            src, dst = xt.at[xs, :, zs], xt.at[xd, :, zd]
        elif ox == 0:
            src, dst = ys.at[side, :, zs], yt.at[side, :, zd]
        else:
            src, dst = ct.at[end, side], ctr.at[end, side, 1 - oz]
        copies.append((src, dst, device))
        if extra is not None and ox != 0 and (oy, oz) == (0, 0):
            source, target = extra
            copies.append((source.at[end], target.at[end], device))
    for src, dst, device in copies:
        remote(src, dst, sems.at[0], sems.at[1], device).start()
    return sum(math.prod(src.shape) * jnp.dtype(src.dtype).itemsize for src, _, _ in copies)


class AllReduce:
    def __init__(self, place, total, fin, r1, s, r2, r3, sems):
        self.place, self.total, self.fin = place, total, fin
        self.r1, self.s, self.r2, self.r3, self.sems = r1, s, r2, r3, sems
        self.half = total.shape[0] // 2
        self.piece = self.half // place.group
        self.step = -1
        self.sizes = (r1, r2, r3.at[pl.ds(0, place.row_group - 1)], r2, s)

    def send(self, src, dst, device):
        remote(src, dst, self.sems.at[0, self.step], self.sems.at[1, self.step], device).start()

    def arrive(self):
        await_bytes(self.sizes[self.step], self.sems.at[1, self.step])
        self.step += 1

    def finish(self):
        self.arrive()
        self.store.wait()
        for step, size in enumerate(self.sizes):
            await_bytes(size, self.sems.at[0, step])

    def mine(self, index, size):
        return pl.ds(pl.multiple_of(index * size, size), size)

    def pair(self, part=0, parts=1):
        p = self.place
        self.step = 0
        size = self.half // parts
        rows = pl.ds(pl.multiple_of((1 - p.core) * self.half + part * size, size), size)
        self.send(self.total.at[rows], self.r1.at[pl.ds(part * size, size)], p.sibling())

    def scatter(self):
        p = self.place
        self.arrive()
        self.s[...] = (self.total[self.mine(p.core, self.half), :] + self.r1[...]).astype(BF16)
        for k, o in enumerate(p.group_steps()):
            device, index = p.in_group(*o)
            self.send(self.s.at[self.mine(index, self.piece)], self.r2.at[k], device)

    def exchange(self):
        p = self.place
        self.arrive()
        total = self.s[self.mine(p.index, self.piece), :].astype(F32)
        for k in range(p.group - 1):
            total = total + self.r2[k].astype(F32)
        self.r3[p.y] = total.astype(BF16)
        for dy in range(1, p.row_group):
            self.send(self.r3.at[p.y], self.r3.at[p.y], p.in_row(dy))

    def spot(self):
        p = self.place
        return pl.ds(pl.multiple_of(p.core * self.half + p.index * self.piece, self.piece), self.piece)

    def gather(self):
        p = self.place
        self.arrive()
        total = self.r3[0].astype(F32)
        for k in range(1, p.row_group):
            total = total + self.r3[k].astype(F32)
        self.fin[self.spot(), :] = total.astype(BF16)
        for o in p.group_steps():
            device, _ = p.in_group(*o)
            self.send(self.fin.at[self.spot()], self.fin.at[self.spot()], device)

    def share(self, out, sem):
        p = self.place
        self.arrive()
        spot = self.mine(p.core, self.half)
        self.send(self.fin.at[spot], out.at[spot], p.sibling())
        self.store = pltpu.make_async_copy(self.fin.at[spot], out.at[spot], sem)
        self.store.start()


def main_kernel(
    sizes, u_in, g_in, wu_in, wc_in,
    coarse_out, out_up, out_conv,
    ub, wu, wc, ue, ue1, uc, uce, xt, ysf, ys, yt, ct, ctr, ctf, yf, yr, ge, ga, gb,
    wp, cw, w3, uw, uwt, pre, slope, ht, gp,
    pxt, pys, pyt, pct, pctr, pyf, pyr, pe, co, gc,
    a_up, a_conv, fin_up, fin_conv, up_r1, up_s, up_r2, up_r3, cv_r1, cv_s, cv_r2, cv_r3,
    local_sems, g_sems, p_sems, up_sems, cv_sems,
):
    place = Place(sizes)
    barrier = pltpu.get_barrier_semaphore()
    partners = [place.neighbour(o) for o in NEIGHBOURS]
    partners += [place.in_group(*o)[0] for o in place.group_steps()]
    partners += [place.in_row(dy) for dy in range(1, place.row_group)]
    partners += [place.sibling()]
    for device in partners[:26]:
        pl.semaphore_signal(barrier, inc=1, device_id=device, device_id_type=MESH)
    loads = [
        pltpu.make_async_copy(u_in, ub, local_sems.at[0]),
        pltpu.make_async_copy(g_in.at[pl.ds(0, 7)], xt.at[pl.ds(3, 7), :, pl.ds(128, 1024)], local_sems.at[1]),
        pltpu.make_async_copy(g_in.at[7], xt.at[12, :, pl.ds(128, 1024)], local_sems.at[2]),
        pltpu.make_async_copy(wu_in, wu, local_sems.at[3]),
        pltpu.make_async_copy(wc_in, wc, local_sems.at[4]),
    ]
    for load in loads:
        load.start()
    for device in partners[26:]:
        pl.semaphore_signal(barrier, inc=1, device_id=device, device_id_type=MESH)

    zero_rows = jnp.zeros((4, 1024), F32)
    for side in range(2):
        ysf[side, 12:16, :] = zero_rows
    loads[0].wait()
    for x in range(4):
        rows = ub[x].astype(F32)
        ue[1 + x, 8:16, 128:640] = rows
        plane = U_PLANES[1 + x]
        for z, lane in ((0, 128), (384, 1024)):
            both = jnp.concatenate([rows[:, z : z + 128], rows[:, z : z + 128]], axis=0)
            xt[plane, :, lane : lane + 128] = both.astype(BF16)
        if x in (0, 3):
            uc[(3 - x) // 3] = jnp.concatenate([rows[:, 0:256], rows[:, 256:512]], axis=0).astype(BF16)
        for side, row in ((0, 7), (1, 0)):
            ysf[side, 8 + x : 9 + x, 0:256] = rows[row : row + 1, 0:256]
            ysf[side, 8 + x : 9 + x, 256:768] = jnp.zeros((1, 512), F32)
            ysf[side, 8 + x : 9 + x, 768:1024] = rows[row : row + 1, 256:512]
    loads[1].wait()
    loads[2].wait()
    for x in range(8):
        block = xt[G_PLANES[1 + x], :, 128:1152].astype(F32)
        ysf[0, x : x + 1, :] = block[15:16]
        ysf[1, x : x + 1, :] = block[0:1]
    for side in range(2):
        ys[side] = ysf[side].astype(BF16)
        for end, x, xc in ((0, 7, 3), (1, 0, 0)):
            ctf[end, side, 0, 8:16, :] = jnp.zeros((8, 128), F32)
            for j in range(8):
                ctf[end, side, 0, j : j + 1, :] = ysf[side, x : x + 1, 128 * j : 128 * j + 128]
            for j, lane in enumerate((0, 128, 768, 896)):
                ctf[end, side, 0, 8 + j : 9 + j, :] = ysf[side, 8 + xc : 9 + xc, lane : lane + 128]
            ct[end, side] = ctf[end, side, 0].astype(BF16)
    pl.semaphore_wait(barrier, len(partners))
    rim_bytes = halo(place, xt, 2, ((12, 0), (3, 15)), (uc, uce), ys, yt, ct, ctr, g_sems)

    loads[3].wait()
    loads[4].wait()
    blank = jnp.zeros((C, C), BF16)
    for q in range(16):
        k0, k1, k2, k3 = (wu[4 * q + k] for k in range(4))
        wp[q, 0:64, :] = jnp.concatenate([k3, blank], axis=1)
        wp[q, 64:128, :] = jnp.concatenate([k1, k2], axis=1)
        wp[q, 128:192, :] = jnp.concatenate([blank, k0], axis=1)
        wp[q, 192:256, :] = jnp.zeros((C, 2 * C), BF16)
        w3[q, :, 0:128] = jnp.concatenate([k0, k1], axis=1)
        w3[q, :, 128:256] = jnp.concatenate([k2, k3], axis=1)
    for dx in range(3):
        for dy in range(3):
            d0, d1, d2 = (wc[9 * dx + 3 * dy + d] for d in range(3))
            tap = jnp.concatenate(
                [
                    jnp.concatenate([d2, d1, d0, blank], axis=1),
                    jnp.concatenate([blank, d2, d1, d0], axis=1),
                ],
                axis=0,
            )
            for py in range(2):
                lane = 256 * (4 * dx + py - dy + 2)
                cw[128 * py : 128 * py + 128, lane : lane + 256] = tap
        cw[128:256, 1024 * dx : 1024 * dx + 256] = jnp.zeros((128, 256), BF16)
        cw[0:128, 1024 * dx + 768 : 1024 * dx + 1024] = jnp.zeros((128, 256), BF16)

    await_bytes(slope.at[pl.ds(0, rim_bytes // 1024)], g_sems.at[1])
    ctf[...] = ctr[...].astype(F32)
    for side in range(2):
        yf[side, 0:16, :] = yt[side].astype(F32)
        for end in range(2):
            for j in range(10):
                tile, row = (0, 7) if j == 0 else (2, 0) if j == 9 else (1, j - 1)
                yf[side, 16 + end : 17 + end, 128 * j : 128 * j + 128] = ctf[end, side, tile, row : row + 1, :]
            for j in range(6):
                tile, row = (0, 11) if j == 0 else (2, 8) if j == 5 else (1, 7 + j)
                ue[5 * end, 7 + 9 * side : 8 + 9 * side, 128 * j : 128 * j + 128] = ctf[
                    end, side, tile, row : row + 1, :
                ]
        for x in range(1, 5):
            row = slice(7 + x, 8 + x)
            ue[x, 7 + 9 * side : 8 + 9 * side, 0:384] = yf[side, row, 0:384]
            ue[x, 7 + 9 * side : 8 + 9 * side, 384:768] = yf[side, row, 896:1280]
    for end in range(2):
        face = uce[end].astype(F32)
        ue[5 * end, 8:16, 128:384] = face[0:8]
        ue[5 * end, 8:16, 384:640] = face[8:16]
    for x in range(6):
        ue[x, 8:16, 0:128] = xt[U_PLANES[x], :, 0:128].astype(F32)[0:8]
        ue[x, 8:16, 640:768] = xt[U_PLANES[x], :, 1152:1280].astype(F32)[0:8]
    for x in range(6):
        ue1[x] = pltpu.roll(ue[x], 768 - 64, 1)[:, :640]
    for sx in range(3):
        for sy in range(3):
            rows = []
            for zc in range(8):
                if zc % 2:
                    part = ue[sx : sx + 4, 7 + sy : 15 + sy, 64 * (zc + 1) : 64 * (zc + 1) + 256]
                else:
                    part = ue1[sx : sx + 4, 7 + sy : 15 + sy, 64 * zc : 64 * zc + 256]
                rows.append(part.reshape(32, 256))
            window = jnp.concatenate(rows, axis=0)
            uw[3 * sx + sy] = window.astype(BF16)
            uwt[3 * sx + sy] = window.T.astype(BF16)[:192]

    for px in range(2):
        for py in range(2):
            total = None
            for sx, kx in taps_by_parity[px]:
                for sy, ky in taps_by_parity[py]:
                    part = nn(uw[3 * sx + sy], wp[4 * kx + ky])
                    total = part if total is None else total + part
            total = total.reshape(8, 4, 8, 128)
            for xc in range(4):
                pre[:, 2 * xc + px, :, 128 * py : 128 * py + 128] = total[:, xc]
    for zc in range(0, 8, 2):
        v = pre[zc : zc + 2].reshape(128, 256)
        square = v * v
        gate = 0.5 + 0.5 * jnp.tanh(v * (gelu_coef + gelu_coef * gelu_cube * square))
        hidden = v * gate
        ht[:, 64 * zc : 64 * zc + 128] = hidden.T.astype(BF16)
        slope[64 * zc : 64 * zc + 128, :] = gate + hidden * (1.0 - gate) * (
            2.0 * gelu_coef + 6.0 * gelu_coef * gelu_cube * square
        )

    turn = xt.shape[2] - 64
    for side in range(2):
        yr[side] = pltpu.roll(yf[side], turn, 1)[:, :1152]
    for x in range(10):
        turned = pltpu.roll(xt[G_PLANES[x]].astype(F32), turn, 1)
        row = 16 if x == 0 else 17 if x == 9 else x - 1
        for pair in range(9):
            lanes = slice(128 * pair, 128 * pair + 128)
            ge[pair, x, 8:24, :] = turned[:, lanes]
            ge[pair, x, 7:8, :] = yr[0, row : row + 1, lanes]
            ge[pair, x, 24:25, :] = yr[1, row : row + 1, lanes]
    for pair in range(9):
        for ky in range(4):
            rows = [ge[pair, x, pl.ds(7 + ky, 8, stride=2), :] for x in range(10)]
            ga[ky, pair] = jnp.concatenate(rows, axis=0).astype(BF16)
            gb[ky, pair] = jnp.concatenate(rows[1:9], axis=0).astype(BF16)

    def window(dx, ky):
        parts = []
        for zc in range(8):
            if dx == 1:
                pairs = [gb[ky, zc + s] for s in range(2)]
            else:
                first = 16 - 8 * dx
                pairs = [ga[ky, zc + s, first : first + 64] for s in range(2)]
            parts.append(jnp.concatenate(pairs, axis=1))
        return jnp.concatenate(parts, axis=0)

    low = lax.broadcasted_iota(jnp.int32, (C, 2 * C), 1) < C
    for dx in range(3):
        products = [
            nn(ht[0:128, :], window(dx, 0)),
            nn(ht[...], window(dx, 1)),
            nn(ht[...], window(dx, 2)),
            nn(ht[128:256, :], window(dx, 3)),
        ]
        for dy in range(3):
            part = products[2 - dy][:128] + products[3 - dy][-128:]
            gc[3 * dx + dy] = part[:64] + pltpu.roll(part[64:], 256 - 64, 1)
    for t in range(9):
        a_conv[64 * t : 64 * t + 64, :] = gc[t, :, 0:128]
    for m in range(5):
        if m < 4:
            other = pltpu.roll(gc[2 * m + 1, :, 128:256], 64, 1)
            joined = jnp.where(low, gc[2 * m, :, 128:256], other)
        else:
            joined = gc[8, :, 128:256]
        a_conv[64 * (9 + m) : 64 * (10 + m), :] = joined
    a_conv[896:1024, :] = jnp.zeros((128, 128), F32)
    conv = AllReduce(place, a_conv, fin_conv, cv_r1, cv_s, cv_r2, cv_r3, cv_sems)
    conv.pair()

    total = None
    for dx in range(3):
        for ky in range(4):
            lane = 256 * (4 * dx + ky)
            part = nt(window(dx, ky), cw[:, lane : lane + 256])
            total = part if total is None else total + part
    gp[...] = (total * slope[...]).astype(BF16).astype(F32).reshape(8, 8, 8, 256)

    conv.scatter()

    up = AllReduce(place, a_up, fin_up, up_r1, up_s, up_r2, up_r3, up_sems)
    for px in range(2):
        rows = [gp[:, 2 * xc + px, :, :] for xc in range(4)]
        grad = jnp.stack(rows, axis=1).reshape(256, 256).astype(BF16)
        product = nn(uwt[3 * px : 3 * px + 6].reshape(1152, 256), grad)
        for i, (sx, _) in enumerate(taps_by_parity[px]):
            for py in range(2):
                for j, (sy, _) in enumerate(taps_by_parity[py]):
                    row = 1024 * i + 512 * px + 256 * py + 128 * j
                    first = 192 * (3 * (sx - px) + sy)
                    part = product[first : first + 192, 128 * py : 128 * py + 128]
                    a_up[row : row + 64, :] = part[64:128]
                    a_up[row + 64 : row + 128, :] = jnp.where(low, part[0:64], part[128:192])
        up.pair(px, 2)

    for x in range(8):
        for zc in range(8):
            block = gp[zc, x]
            rows = jnp.concatenate([block[:, 0:128], block[:, 128:256]], axis=0)
            pxt[1 + x, :, 128 * zc + 128 : 128 * zc + 256] = rows.astype(BF16)
            pys[0, x : x + 1, 128 * zc : 128 * zc + 128] = gp[zc, x, 7:8, 128:256]
            pys[1, x : x + 1, 128 * zc : 128 * zc + 128] = gp[zc, x, 0:1, 0:128]
            if x in (0, 7):
                pct[(7 - x) // 7, 0, zc : zc + 1, :] = gp[zc, x, 7:8, 128:256]
                pct[(7 - x) // 7, 1, zc : zc + 1, :] = gp[zc, x, 0:1, 0:128]
    up.scatter()
    conv.exchange()
    p_bytes = halo(place, pxt, 1, ((8, 0), (1, 9)), None, pys, pyt, pct, pctr, p_sems)
    up.exchange()
    conv.gather()
    up.gather()

    await_bytes(slope.at[pl.ds(0, p_bytes // 1024)], p_sems.at[1])
    for side in range(2):
        pyf[side, 0:8, :] = pyt[side]
        for end in range(2):
            for j in range(10):
                tile, row = (0, 7) if j == 0 else (2, 0) if j == 9 else (1, j - 1)
                pyf[side, 8 + end : 9 + end, 128 * j : 128 * j + 128] = pctr[end, side, tile, row : row + 1, :]
        pyr[side] = pltpu.roll(pyf[side], turn, 1)[:, :1152]
    for x in range(10):
        turned = pltpu.roll(pxt[x].astype(F32), turn, 1)
        row = 8 if x == 0 else 9 if x == 9 else x - 1
        for pair in range(9):
            lanes = slice(128 * pair, 128 * pair + 128)
            pe[pair, x, 0, 8:16, :] = turned[0:8, lanes]
            pe[pair, x, 1, 8:16, :] = turned[8:16, lanes]
            pe[pair, x, 0, 16:17, :] = pyr[1, row : row + 1, lanes]
            pe[pair, x, 1, 7:8, :] = pyr[0, row : row + 1, lanes]
    total = None
    for kx in range(4):
        for ky in range(4):
            parity, first = ((1, 7), (0, 8), (1, 8), (0, 9))[ky]
            pairs = [
                jnp.concatenate([pe[pair, 2 * xc + kx, parity, first : first + 8, :] for xc in range(4)], axis=0)
                for pair in range(9)
            ]
            rows = [jnp.concatenate([pairs[zc], pairs[zc + 1]], axis=1) for zc in range(8)]
            part = nt(jnp.concatenate(rows, axis=0).astype(BF16), w3[4 * kx + ky])
            total = part if total is None else total + part
    total = total.reshape(8, 4, 8, C)
    for zc in range(0, 8, 2):
        co[:, :, 64 * zc : 64 * zc + 128] = jnp.concatenate([total[zc], total[zc + 1]], axis=2).astype(BF16)
    store = pltpu.make_async_copy(co, coarse_out, local_sems.at[5])
    store.start()
    conv.share(out_conv, local_sems.at[6])
    up.share(out_up, local_sems.at[7])
    up.finish()
    conv.finish()
    store.wait()
    await_bytes(slope.at[pl.ds(0, rim_bytes // 1024)], g_sems.at[0])
    await_bytes(slope.at[pl.ds(0, p_bytes // 1024)], p_sems.at[0])


def last_kernel(
    factor, coarse, in_up, in_conv, coarse_out, up_out, conv_out, fin_up, fin_conv, up, conv, in_sems, out_sems
):
    through = pltpu.make_async_copy(coarse, coarse_out, out_sems.at[5])
    through.start()
    parts = [pl.ds(512 * i, 512) for i in range(4)]
    loads = [pltpu.make_async_copy(in_up.at[p], fin_up.at[p], in_sems.at[i]) for i, p in enumerate(parts)]
    loads.append(pltpu.make_async_copy(in_conv, fin_conv, in_sems.at[4]))
    for load in loads:
        load.start()
    stores = []
    for i in range(4):
        loads[i].wait()
        for s in range(4 * i, 4 * i + 4):
            half, px, py, j = s // 8, s // 4 % 2, s // 2 % 2, s % 2
            q = 4 * taps_by_parity[px][half][1] + taps_by_parity[py][j][1]
            first = fin_up[128 * s : 128 * s + 64, :].astype(F32) * factor
            second = fin_up[128 * s + 64 : 128 * s + 128, :].astype(F32) * factor
            up[4 * q + 1] = first[:, :C]
            up[4 * q + 2] = first[:, C:]
            up[4 * q + 3] = second[:, :C]
            up[4 * q] = second[:, C:]
        kx = taps_by_parity[i % 2][i // 2][1]
        part = pl.ds(16 * kx, 16)
        stores.append(pltpu.make_async_copy(up.at[part], up_out.at[part], out_sems.at[i]))
        stores[-1].start()
    loads[4].wait()
    for t in range(9):
        both = fin_conv[64 * t : 64 * t + 64, :].astype(F32) * factor
        conv[3 * t + 2] = both[:, :C]
        conv[3 * t + 1] = both[:, C:]
        m = t // 2
        rest = fin_conv[64 * (9 + m) : 64 * (10 + m), :].astype(F32) * factor
        conv[3 * t] = rest[:, C:] if t % 2 else rest[:, :C]
    stores.append(pltpu.make_async_copy(conv, conv_out, out_sems.at[4]))
    stores[-1].start()
    for store in stores:
        store.wait()
    through.wait()


def local(sizes, coarse_in, out_grad, up_weight, conv_weight):
    every_cell = 2048 * sizes[0] * sizes[1] * sizes[2]
    group = sizes[0] // 2 * sizes[1]
    row_group = sizes[2] // 2 * 2
    up_piece, cv_piece = 1024 // group, 512 // group
    vmem = pltpu.VMEM
    dma = pltpu.SemaphoreType.DMA
    anywhere = pl.BlockSpec(memory_space=pl.ANY)
    scratch = [
        vmem((4, 8, 512), BF16), vmem((64, C, C), BF16), vmem((27, C, C), BF16),
        vmem((6, 24, 768), F32), vmem((6, 24, 640), F32), vmem((2, 16, 256), BF16), vmem((2, 16, 256), BF16),
        vmem((16, 16, 1280), BF16), vmem((2, 16, 1024), F32), vmem((2, 16, 1024), BF16),
        vmem((2, 16, 1280), BF16), vmem((2, 2, 16, 128), BF16), vmem((2, 2, 3, 16, 128), BF16),
        vmem((2, 2, 3, 16, 128), F32), vmem((2, 24, 1280), F32), vmem((2, 24, 1152), F32),
        vmem((9, 10, 32, 128), F32), vmem((4, 9, 80, 128), BF16), vmem((4, 9, 64, 128), BF16),
        vmem((16, 256, 128), BF16), vmem((256, 3072), BF16), vmem((16, 64, 256), BF16),
        vmem((9, 256, 256), BF16), vmem((9, 192, 256), BF16),
        vmem((8, 8, 8, 256), F32), vmem((512, 256), F32), vmem((256, 512), BF16), vmem((8, 8, 8, 256), F32),
        vmem((10, 16, 1280), BF16), vmem((2, 8, 1024), F32), vmem((2, 8, 1280), F32),
        vmem((2, 2, 8, 128), F32), vmem((2, 2, 3, 8, 128), F32), vmem((2, 16, 1280), F32),
        vmem((2, 16, 1152), F32), vmem((9, 10, 2, 24, 128), F32), vmem((4, 8, 512), BF16),
        vmem((9, 64, 256), F32),
        vmem((2048, 128), F32), vmem((1024, 128), F32), vmem((2048, 128), BF16), vmem((1024, 128), BF16),
        vmem((1024, 128), F32), vmem((1024, 128), BF16), vmem((group - 1, up_piece, 128), BF16),
        vmem((row_group, up_piece, 128), BF16),
        vmem((512, 128), F32), vmem((512, 128), BF16), vmem((group - 1, cv_piece, 128), BF16),
        vmem((row_group, cv_piece, 128), BF16),
        dma((8,)), dma((2,)), dma((2,)), dma((2, 5)), dma((2, 5)),
    ]
    coarse, fin_up, fin_conv = pl.pallas_call(
        functools.partial(main_kernel, sizes),
        name="halo_compute_reduce",
        out_shape=(
            jax.ShapeDtypeStruct((4, 8, 512), BF16),
            jax.ShapeDtypeStruct((2048, 128), BF16),
            jax.ShapeDtypeStruct((1024, 128), BF16),
        ),
        in_specs=[anywhere] * 4,
        out_specs=(anywhere,) * 3,
        scratch_shapes=scratch,
        compiler_params=pltpu.CompilerParams(
            collective_id=0, has_side_effects=True, vmem_limit_bytes=60 * 2**20
        ),
    )(coarse_in, out_grad, up_weight, conv_weight)
    return pl.pallas_call(
        functools.partial(last_kernel, 1.0 / math.sqrt(every_cell)),
        name="scale_outputs",
        out_shape=(
            jax.ShapeDtypeStruct((4, 8, 512), BF16),
            jax.ShapeDtypeStruct((64, C, C), F32),
            jax.ShapeDtypeStruct((27, C, C), F32),
        ),
        in_specs=[anywhere] * 3,
        out_specs=(anywhere,) * 3,
        scratch_shapes=[
            vmem((2048, 128), BF16), vmem((1024, 128), BF16), vmem((64, C, C), F32), vmem((27, C, C), F32),
            dma((5,)), dma((6,)),
        ],
        compiler_params=pltpu.CompilerParams(vmem_limit_bytes=60 * 2**20),
    )(coarse, fin_up, fin_conv)


def solution(mesh):
    sizes = tuple(mesh.shape[a] for a in ("gx", "gy", "gz"))
    in_specs = (P("gx", "gy", "gz"), P("gx", "gy", "gz"), P(), P())
    out_specs = (P("gx", "gy", "gz"), P(), P())
    return jax.shard_map(
        functools.partial(local, sizes), mesh=mesh, in_specs=in_specs, out_specs=out_specs, check_vma=False
    )
```

```python
import functools
import itertools
import math

import jax
import jax.numpy as jnp
from jax import lax
from jax.experimental import pallas as pl
from jax.experimental.pallas import tpu as pltpu
from jax.sharding import PartitionSpec as P

MESH = pl.DeviceIdType.MESH
F32 = jnp.float32
BF16 = jnp.bfloat16
C = 64
gelu_coef = 0.7978845608
gelu_cube = 0.044715
taps_by_parity = (((0, 3), (1, 1)), ((1, 2), (2, 0)))
NEIGHBOURS = sorted((o for o in itertools.product((-1, 0, 1), repeat=3) if any(o)), key=lambda o: (-abs(o[0]), sum(map(abs, o))))
G_PLANES = [0, 3, 4, 5, 6, 7, 8, 9, 12, 15]
U_PLANES = [1, 2, 10, 11, 13, 14]


def nt(left, right):
    return lax.dot_general(left, right, (((1,), (1,)), ((), ())), preferred_element_type=F32)


def nn(left, right):
    return jnp.dot(left, right, preferred_element_type=F32)


class Place:
    def __init__(self, sizes):
        self.sizes = sizes
        self.gx, self.gy, self.gz = (lax.axis_index(a) for a in ("gx", "gy", "gz"))
        self.nz, self.nx, self.ny = sizes[0] // 2, sizes[1], sizes[2]
        self.low = sizes[2] // 2
        self.z, self.x = self.gx // 2, self.gy
        self.y = self.gx % 2 * self.low + self.gz // 2
        self.core = self.gz % 2
        self.index = self.z * self.nx + self.x
        self.group = self.nz * self.nx
        self.row_group = 2 * self.low

    def neighbour(self, o):
        me = (self.gx, self.gy, self.gz)
        return tuple(lax.rem(m + d + n, n) for m, d, n in zip(me, o, self.sizes))

    def sibling(self):
        return (self.gx, self.gy, self.gz + 1 - 2 * self.core)

    def in_group(self, dz, dx):
        z, x = lax.rem(self.z + dz, self.nz), lax.rem(self.x + dx, self.nx)
        return (z * 2 + self.gx % 2, x, self.gz), z * self.nx + x

    def in_row(self, dy):
        y = lax.rem(self.y + dy, self.row_group)
        return (self.z * 2 + y // self.low, self.x, y % self.low * 2 + self.core)

    def group_steps(self):
        far = lambda o: -min(o[0], self.nz - o[0]) - min(o[1], self.nx - o[1])
        return sorted((o for o in itertools.product(range(self.nz), range(self.nx)) if any(o)), key=far)


def remote(src, dst, send, recv, device):
    return pltpu.make_async_remote_copy(
        src_ref=src, dst_ref=dst, send_sem=send, recv_sem=recv, device_id=device, device_id_type=MESH
    )


def await_bytes(ref, sem):
    pltpu.make_async_copy(ref, ref, sem).wait()


def halo(place, xt, edge, faces, extra, ys, yt, ct, ctr, sems):
    copies = []
    planes, lanes = xt.shape[0], xt.shape[2] - 256
    inner = planes - 2 * edge
    for ox, oy, oz in NEIGHBOURS:
        device = place.neighbour((ox, oy, oz))
        zs, zd = {
            0: (pl.ds(0, lanes), pl.ds(128, lanes)),
            1: (pl.ds(lanes - 128, 128), pl.ds(0, 128)),
            -1: (pl.ds(0, 128), pl.ds(lanes + 128, 128)),
        }[oz]
        side, end = (1 - oy) // 2, (1 - ox) // 2
        if oy == 0:
            zs = pl.ds(zs.start + 128, zs.size)
            if ox == 0:
                xs, xd = pl.ds(edge, inner), pl.ds(edge, inner)
            elif oz == 0:
                xs, xd = faces[end]
            else:
                xs, xd = (
                    (pl.ds(inner, edge), pl.ds(0, edge)),
                    (pl.ds(edge, edge), pl.ds(planes - edge, edge)),
                )[end]
            src, dst = xt.at[xs, :, zs], xt.at[xd, :, zd]
        elif ox == 0:
            src, dst = ys.at[side, :, zs], yt.at[side, :, zd]
        else:
            src, dst = ct.at[end, side], ctr.at[end, side, 1 - oz]
        copies.append((src, dst, device))
        if extra is not None and ox != 0 and (oy, oz) == (0, 0):
            source, target = extra
            copies.append((source.at[end], target.at[end], device))
    for src, dst, device in copies:
        remote(src, dst, sems.at[0], sems.at[1], device).start()
    return sum(math.prod(src.shape) * jnp.dtype(src.dtype).itemsize for src, _, _ in copies)


class AllReduce:
    def __init__(self, place, total, rounded, fin, r1, s, r2, r3, sems):
        self.place, self.total, self.rounded, self.fin = place, total, rounded, fin
        self.r1, self.s, self.r2, self.r3, self.sems = r1, s, r2, r3, sems
        self.half = total.shape[0] // 2
        self.piece = self.half // place.group
        self.step = -1
        self.sizes = (r1, r2, r3.at[pl.ds(0, place.row_group - 1)], r2, s)

    def send(self, src, dst, device):
        remote(src, dst, self.sems.at[0, self.step], self.sems.at[1, self.step], device).start()

    def arrive(self):
        await_bytes(self.sizes[self.step], self.sems.at[1, self.step])
        self.step += 1

    def finish(self):
        self.arrive()
        self.store.wait()
        for step, size in enumerate(self.sizes):
            await_bytes(size, self.sems.at[0, step])

    def mine(self, index, size):
        return pl.ds(pl.multiple_of(index * size, size), size)

    def pair(self, part=0, parts=1):
        p = self.place
        self.step = 0
        size = self.half // parts
        rows = pl.ds(pl.multiple_of((1 - p.core) * self.half + part * size, size), size)
        self.send(self.rounded.at[rows], self.r1.at[pl.ds(part * size, size)], p.sibling())

    def scatter(self):
        p = self.place
        self.arrive()
        self.s[...] = (self.total[self.mine(p.core, self.half), :] + self.r1[...].astype(F32)).astype(BF16)
        for k, o in enumerate(p.group_steps()):
            device, index = p.in_group(*o)
            self.send(self.s.at[self.mine(index, self.piece)], self.r2.at[k], device)

    def exchange(self):
        p = self.place
        self.arrive()
        total = self.s[self.mine(p.index, self.piece), :].astype(F32)
        for k in range(p.group - 1):
            total = total + self.r2[k].astype(F32)
        self.r3[p.y] = total.astype(BF16)
        for dy in sorted(range(1, p.row_group), key=lambda d: -min(d, p.row_group - d)):
            self.send(self.r3.at[p.y], self.r3.at[p.y], p.in_row(dy))

    def spot(self):
        p = self.place
        return pl.ds(pl.multiple_of(p.core * self.half + p.index * self.piece, self.piece), self.piece)

    def gather(self):
        p = self.place
        self.arrive()
        total = self.r3[0].astype(F32)
        for k in range(1, p.row_group):
            total = total + self.r3[k].astype(F32)
        self.fin[self.spot(), :] = total.astype(BF16)
        for o in p.group_steps():
            device, _ = p.in_group(*o)
            self.send(self.fin.at[self.spot()], self.fin.at[self.spot()], device)

    def share(self, out, sem):
        p = self.place
        self.arrive()
        spot = self.mine(p.core, self.half)
        self.send(self.fin.at[spot], out.at[spot], p.sibling())
        self.store = pltpu.make_async_copy(self.fin.at[spot], out.at[spot], sem)
        self.store.start()


def main_kernel(
    sizes, u_in, g_in, wu_in, wc_in,
    coarse_out, out_up, out_conv,
    ub, wu, wc, ue, ue1, uc, uce, xt, ysf, ys, yt, ct, ctr, ctf, yf, yr, ge, ga, gb,
    wp, cw, w3, uw, uwt, pre, slope, ht, gp,
    pxt, pys, pyt, pct, pctr, pyf, pyr, pe, co, gc,
    a_up, a_conv, b_up, b_conv, fin_up, fin_conv, up_r1, up_s, up_r2, up_r3, cv_r1, cv_s, cv_r2, cv_r3,
    local_sems, g_sems, p_sems, up_sems, cv_sems,
):
    place = Place(sizes)
    barrier = pltpu.get_barrier_semaphore()
    partners = [place.neighbour(o) for o in NEIGHBOURS]
    partners += [place.in_group(*o)[0] for o in place.group_steps()]
    partners += [place.in_row(dy) for dy in range(1, place.row_group)]
    partners += [place.sibling()]
    for device in partners[:26]:
        pl.semaphore_signal(barrier, inc=1, device_id=device, device_id_type=MESH)
    loads = [
        pltpu.make_async_copy(u_in, ub, local_sems.at[0]),
        pltpu.make_async_copy(g_in.at[pl.ds(0, 7)], xt.at[pl.ds(3, 7), :, pl.ds(128, 1024)], local_sems.at[1]),
        pltpu.make_async_copy(g_in.at[7], xt.at[12, :, pl.ds(128, 1024)], local_sems.at[2]),
        pltpu.make_async_copy(wu_in, wu, local_sems.at[3]),
        pltpu.make_async_copy(wc_in, wc, local_sems.at[4]),
    ]
    for load in loads:
        load.start()
    for device in partners[26:]:
        pl.semaphore_signal(barrier, inc=1, device_id=device, device_id_type=MESH)

    zero_rows = jnp.zeros((4, 1024), F32)
    for side in range(2):
        ysf[side, 12:16, :] = zero_rows
    loads[0].wait()
    for x in range(4):
        rows = ub[x].astype(F32)
        ue[1 + x, 8:16, 128:640] = rows
        plane = U_PLANES[1 + x]
        for z, lane in ((0, 128), (384, 1024)):
            both = jnp.concatenate([rows[:, z : z + 128], rows[:, z : z + 128]], axis=0)
            xt[plane, :, lane : lane + 128] = both.astype(BF16)
        if x in (0, 3):
            uc[(3 - x) // 3] = jnp.concatenate([rows[:, 0:256], rows[:, 256:512]], axis=0).astype(BF16)
        for side, row in ((0, 7), (1, 0)):
            ysf[side, 8 + x : 9 + x, 0:256] = rows[row : row + 1, 0:256]
            ysf[side, 8 + x : 9 + x, 256:768] = jnp.zeros((1, 512), F32)
            ysf[side, 8 + x : 9 + x, 768:1024] = rows[row : row + 1, 256:512]
    loads[1].wait()
    loads[2].wait()
    for x in range(8):
        block = xt[G_PLANES[1 + x], :, 128:1152].astype(F32)
        ysf[0, x : x + 1, :] = block[15:16]
        ysf[1, x : x + 1, :] = block[0:1]
    for side in range(2):
        ys[side] = ysf[side].astype(BF16)
        for end, x, xc in ((0, 7, 3), (1, 0, 0)):
            ctf[end, side, 0, 8:16, :] = jnp.zeros((8, 128), F32)
            for j in range(8):
                ctf[end, side, 0, j : j + 1, :] = ysf[side, x : x + 1, 128 * j : 128 * j + 128]
            for j, lane in enumerate((0, 128, 768, 896)):
                ctf[end, side, 0, 8 + j : 9 + j, :] = ysf[side, 8 + xc : 9 + xc, lane : lane + 128]
            ct[end, side] = ctf[end, side, 0].astype(BF16)
    pl.semaphore_wait(barrier, len(partners))
    rim_bytes = halo(place, xt, 2, ((12, 0), (3, 15)), (uc, uce), ys, yt, ct, ctr, g_sems)

    loads[3].wait()
    loads[4].wait()
    blank = jnp.zeros((C, C), BF16)
    for q in range(16):
        k0, k1, k2, k3 = (wu[4 * q + k] for k in range(4))
        wp[q, 0:64, :] = jnp.concatenate([k3, blank], axis=1)
        wp[q, 64:128, :] = jnp.concatenate([k1, k2], axis=1)
        wp[q, 128:192, :] = jnp.concatenate([blank, k0], axis=1)
        wp[q, 192:256, :] = jnp.zeros((C, 2 * C), BF16)
        w3[q, :, 0:128] = jnp.concatenate([k0, k1], axis=1)
        w3[q, :, 128:256] = jnp.concatenate([k2, k3], axis=1)
    for dx in range(3):
        for dy in range(3):
            d0, d1, d2 = (wc[9 * dx + 3 * dy + d] for d in range(3))
            tap = jnp.concatenate(
                [
                    jnp.concatenate([d2, d1, d0, blank], axis=1),
                    jnp.concatenate([blank, d2, d1, d0], axis=1),
                ],
                axis=0,
            )
            for py in range(2):
                lane = 256 * (4 * dx + py - dy + 2)
                cw[128 * py : 128 * py + 128, lane : lane + 256] = tap
        cw[128:256, 1024 * dx : 1024 * dx + 256] = jnp.zeros((128, 256), BF16)
        cw[0:128, 1024 * dx + 768 : 1024 * dx + 1024] = jnp.zeros((128, 256), BF16)

    await_bytes(slope.at[pl.ds(0, rim_bytes // 1024)], g_sems.at[1])
    ctf[...] = ctr[...].astype(F32)
    for side in range(2):
        yf[side, 0:16, :] = yt[side].astype(F32)
        for end in range(2):
            for j in range(10):
                tile, row = (0, 7) if j == 0 else (2, 0) if j == 9 else (1, j - 1)
                yf[side, 16 + end : 17 + end, 128 * j : 128 * j + 128] = ctf[end, side, tile, row : row + 1, :]
            for j in range(6):
                tile, row = (0, 11) if j == 0 else (2, 8) if j == 5 else (1, 7 + j)
                ue[5 * end, 7 + 9 * side : 8 + 9 * side, 128 * j : 128 * j + 128] = ctf[
                    end, side, tile, row : row + 1, :
                ]
        for x in range(1, 5):
            row = slice(7 + x, 8 + x)
            ue[x, 7 + 9 * side : 8 + 9 * side, 0:384] = yf[side, row, 0:384]
            ue[x, 7 + 9 * side : 8 + 9 * side, 384:768] = yf[side, row, 896:1280]
    for end in range(2):
        face = uce[end].astype(F32)
        ue[5 * end, 8:16, 128:384] = face[0:8]
        ue[5 * end, 8:16, 384:640] = face[8:16]
    for x in range(6):
        ue[x, 8:16, 0:128] = xt[U_PLANES[x], :, 0:128].astype(F32)[0:8]
        ue[x, 8:16, 640:768] = xt[U_PLANES[x], :, 1152:1280].astype(F32)[0:8]
    for x in range(6):
        ue1[x] = pltpu.roll(ue[x], 768 - 64, 1)[:, :640]
    for sx in range(3):
        for sy in range(3):
            rows = []
            for zc in range(8):
                if zc % 2:
                    part = ue[sx : sx + 4, 7 + sy : 15 + sy, 64 * (zc + 1) : 64 * (zc + 1) + 256]
                else:
                    part = ue1[sx : sx + 4, 7 + sy : 15 + sy, 64 * zc : 64 * zc + 256]
                rows.append(part.reshape(32, 256))
            window = jnp.concatenate(rows, axis=0)
            uw[3 * sx + sy] = window.astype(BF16)
            uwt[3 * sx + sy] = window.T.astype(BF16)[:192]

    for px in range(2):
        for py in range(2):
            total = None
            for sx, kx in taps_by_parity[px]:
                for sy, ky in taps_by_parity[py]:
                    part = nn(uw[3 * sx + sy], wp[4 * kx + ky])
                    total = part if total is None else total + part
            total = total.reshape(8, 4, 8, 128)
            for xc in range(4):
                pre[:, 2 * xc + px, :, 128 * py : 128 * py + 128] = total[:, xc]
    for zc in range(0, 8, 2):
        v = pre[zc : zc + 2].reshape(128, 256)
        square = v * v
        gate = 0.5 + 0.5 * jnp.tanh(v * (gelu_coef + gelu_coef * gelu_cube * square))
        hidden = v * gate
        ht[:, 64 * zc : 64 * zc + 128] = hidden.T.astype(BF16)
        slope[64 * zc : 64 * zc + 128, :] = gate + hidden * (1.0 - gate) * (
            2.0 * gelu_coef + 6.0 * gelu_coef * gelu_cube * square
        )

    turn = xt.shape[2] - 64
    for side in range(2):
        yr[side] = pltpu.roll(yf[side], turn, 1)[:, :1152]
    for x in range(10):
        turned = pltpu.roll(xt[G_PLANES[x]].astype(F32), turn, 1)
        row = 16 if x == 0 else 17 if x == 9 else x - 1
        for pair in range(9):
            lanes = slice(128 * pair, 128 * pair + 128)
            ge[pair, x, 8:24, :] = turned[:, lanes]
            ge[pair, x, 7:8, :] = yr[0, row : row + 1, lanes]
            ge[pair, x, 24:25, :] = yr[1, row : row + 1, lanes]
    for pair in range(9):
        for ky in range(4):
            rows = [ge[pair, x, pl.ds(7 + ky, 8, stride=2), :] for x in range(10)]
            ga[ky, pair] = jnp.concatenate(rows, axis=0).astype(BF16)
            gb[ky, pair] = jnp.concatenate(rows[1:9], axis=0).astype(BF16)

    def window(dx, ky):
        parts = []
        for zc in range(8):
            if dx == 1:
                pairs = [gb[ky, zc + s] for s in range(2)]
            else:
                first = 16 - 8 * dx
                pairs = [ga[ky, zc + s, first : first + 64] for s in range(2)]
            parts.append(jnp.concatenate(pairs, axis=1))
        return jnp.concatenate(parts, axis=0)

    low = lax.broadcasted_iota(jnp.int32, (C, 2 * C), 1) < C
    for dx in range(3):
        products = [
            nn(ht[0:128, :], window(dx, 0)),
            nn(ht[...], window(dx, 1)),
            nn(ht[...], window(dx, 2)),
            nn(ht[128:256, :], window(dx, 3)),
        ]
        for dy in range(3):
            part = products[2 - dy][:128] + products[3 - dy][-128:]
            gc[3 * dx + dy] = part[:64] + pltpu.roll(part[64:], 256 - 64, 1)
    for t in range(9):
        a_conv[64 * t : 64 * t + 64, :] = gc[t, :, 0:128]
    for m in range(5):
        if m < 4:
            other = pltpu.roll(gc[2 * m + 1, :, 128:256], 64, 1)
            joined = jnp.where(low, gc[2 * m, :, 128:256], other)
        else:
            joined = gc[8, :, 128:256]
        a_conv[64 * (9 + m) : 64 * (10 + m), :] = joined
    a_conv[896:1024, :] = jnp.zeros((128, 128), F32)
    b_conv[...] = a_conv[...].astype(BF16)
    conv = AllReduce(place, a_conv, b_conv, fin_conv, cv_r1, cv_s, cv_r2, cv_r3, cv_sems)
    conv.pair()

    total = None
    for dx in range(3):
        for ky in range(4):
            lane = 256 * (4 * dx + ky)
            part = nt(window(dx, ky), cw[:, lane : lane + 256])
            total = part if total is None else total + part
    gp[...] = (total * slope[...]).astype(BF16).astype(F32).reshape(8, 8, 8, 256)

    conv.scatter()

    up = AllReduce(place, a_up, b_up, fin_up, up_r1, up_s, up_r2, up_r3, up_sems)
    for px in range(2):
        rows = [gp[:, 2 * xc + px, :, :] for xc in range(4)]
        grad = jnp.stack(rows, axis=1).reshape(256, 256).astype(BF16)
        product = nn(uwt[3 * px : 3 * px + 6].reshape(1152, 256), grad)
        for i, (sx, _) in enumerate(taps_by_parity[px]):
            for py in range(2):
                for j, (sy, _) in enumerate(taps_by_parity[py]):
                    row = 1024 * i + 512 * px + 256 * py + 128 * j
                    first = 192 * (3 * (sx - px) + sy)
                    part = product[first : first + 192, 128 * py : 128 * py + 128]
                    outer = jnp.where(low, part[0:64], part[128:192])
                    a_up[row : row + 64, :] = part[64:128]
                    a_up[row + 64 : row + 128, :] = outer
                    b_up[row : row + 64, :] = part[64:128].astype(BF16)
                    b_up[row + 64 : row + 128, :] = outer.astype(BF16)
        up.pair(px, 2)

    for x in range(8):
        for zc in range(8):
            block = gp[zc, x]
            rows = jnp.concatenate([block[:, 0:128], block[:, 128:256]], axis=0)
            pxt[1 + x, :, 128 * zc + 128 : 128 * zc + 256] = rows.astype(BF16)
            pys[0, x : x + 1, 128 * zc : 128 * zc + 128] = gp[zc, x, 7:8, 128:256]
            pys[1, x : x + 1, 128 * zc : 128 * zc + 128] = gp[zc, x, 0:1, 0:128]
            if x in (0, 7):
                pct[(7 - x) // 7, 0, zc : zc + 1, :] = gp[zc, x, 7:8, 128:256]
                pct[(7 - x) // 7, 1, zc : zc + 1, :] = gp[zc, x, 0:1, 0:128]
    up.scatter()
    conv.exchange()
    p_bytes = halo(place, pxt, 1, ((8, 0), (1, 9)), None, pys, pyt, pct, pctr, p_sems)
    up.exchange()
    conv.gather()
    up.gather()

    await_bytes(slope.at[pl.ds(0, p_bytes // 1024)], p_sems.at[1])
    for side in range(2):
        pyf[side, 0:8, :] = pyt[side]
        for end in range(2):
            for j in range(10):
                tile, row = (0, 7) if j == 0 else (2, 0) if j == 9 else (1, j - 1)
                pyf[side, 8 + end : 9 + end, 128 * j : 128 * j + 128] = pctr[end, side, tile, row : row + 1, :]
        pyr[side] = pltpu.roll(pyf[side], turn, 1)[:, :1152]
    for x in range(10):
        turned = pltpu.roll(pxt[x].astype(F32), turn, 1)
        row = 8 if x == 0 else 9 if x == 9 else x - 1
        for pair in range(9):
            lanes = slice(128 * pair, 128 * pair + 128)
            pe[pair, x, 0, 8:16, :] = turned[0:8, lanes]
            pe[pair, x, 1, 8:16, :] = turned[8:16, lanes]
            pe[pair, x, 0, 16:17, :] = pyr[1, row : row + 1, lanes]
            pe[pair, x, 1, 7:8, :] = pyr[0, row : row + 1, lanes]
    total = None
    for kx in range(4):
        for ky in range(4):
            parity, first = ((1, 7), (0, 8), (1, 8), (0, 9))[ky]
            pairs = [
                jnp.concatenate([pe[pair, 2 * xc + kx, parity, first : first + 8, :] for xc in range(4)], axis=0)
                for pair in range(9)
            ]
            rows = [jnp.concatenate([pairs[zc], pairs[zc + 1]], axis=1) for zc in range(8)]
            part = nt(jnp.concatenate(rows, axis=0).astype(BF16), w3[4 * kx + ky])
            total = part if total is None else total + part
    total = total.reshape(8, 4, 8, C)
    for zc in range(0, 8, 2):
        co[:, :, 64 * zc : 64 * zc + 128] = jnp.concatenate([total[zc], total[zc + 1]], axis=2).astype(BF16)
    store = pltpu.make_async_copy(co, coarse_out, local_sems.at[5])
    store.start()
    conv.share(out_conv, local_sems.at[6])
    up.share(out_up, local_sems.at[7])
    up.finish()
    conv.finish()
    store.wait()
    await_bytes(slope.at[pl.ds(0, rim_bytes // 1024)], g_sems.at[0])
    await_bytes(slope.at[pl.ds(0, p_bytes // 1024)], p_sems.at[0])


def last_kernel(
    factor, coarse, in_up, in_conv, coarse_out, up_out, conv_out, fin_up, fin_conv, up, conv, in_sems, out_sems
):
    through = pltpu.make_async_copy(coarse, coarse_out, out_sems.at[5])
    through.start()
    parts = [pl.ds(512 * i, 512) for i in range(4)]
    loads = [pltpu.make_async_copy(in_up.at[p], fin_up.at[p], in_sems.at[i]) for i, p in enumerate(parts)]
    loads.append(pltpu.make_async_copy(in_conv, fin_conv, in_sems.at[4]))
    for load in loads:
        load.start()
    stores = []
    for i in range(4):
        loads[i].wait()
        for s in range(4 * i, 4 * i + 4):
            half, px, py, j = s // 8, s // 4 % 2, s // 2 % 2, s % 2
            q = 4 * taps_by_parity[px][half][1] + taps_by_parity[py][j][1]
            first = fin_up[128 * s : 128 * s + 64, :].astype(F32) * factor
            second = fin_up[128 * s + 64 : 128 * s + 128, :].astype(F32) * factor
            up[4 * q + 1] = first[:, :C]
            up[4 * q + 2] = first[:, C:]
            up[4 * q + 3] = second[:, :C]
            up[4 * q] = second[:, C:]
        kx = taps_by_parity[i % 2][i // 2][1]
        part = pl.ds(16 * kx, 16)
        stores.append(pltpu.make_async_copy(up.at[part], up_out.at[part], out_sems.at[i]))
        stores[-1].start()
    loads[4].wait()
    for t in range(9):
        both = fin_conv[64 * t : 64 * t + 64, :].astype(F32) * factor
        conv[3 * t + 2] = both[:, :C]
        conv[3 * t + 1] = both[:, C:]
        m = t // 2
        rest = fin_conv[64 * (9 + m) : 64 * (10 + m), :].astype(F32) * factor
        conv[3 * t] = rest[:, C:] if t % 2 else rest[:, :C]
    stores.append(pltpu.make_async_copy(conv, conv_out, out_sems.at[4]))
    stores[-1].start()
    for store in stores:
        store.wait()
    through.wait()


def local(sizes, coarse_in, out_grad, up_weight, conv_weight):
    every_cell = 2048 * sizes[0] * sizes[1] * sizes[2]
    group = sizes[0] // 2 * sizes[1]
    row_group = sizes[2] // 2 * 2
    up_piece, cv_piece = 1024 // group, 512 // group
    vmem = pltpu.VMEM
    dma = pltpu.SemaphoreType.DMA
    anywhere = pl.BlockSpec(memory_space=pl.ANY)
    scratch = [
        vmem((4, 8, 512), BF16), vmem((64, C, C), BF16), vmem((27, C, C), BF16),
        vmem((6, 24, 768), F32), vmem((6, 24, 640), F32), vmem((2, 16, 256), BF16), vmem((2, 16, 256), BF16),
        vmem((16, 16, 1280), BF16), vmem((2, 16, 1024), F32), vmem((2, 16, 1024), BF16),
        vmem((2, 16, 1280), BF16), vmem((2, 2, 16, 128), BF16), vmem((2, 2, 3, 16, 128), BF16),
        vmem((2, 2, 3, 16, 128), F32), vmem((2, 24, 1280), F32), vmem((2, 24, 1152), F32),
        vmem((9, 10, 32, 128), F32), vmem((4, 9, 80, 128), BF16), vmem((4, 9, 64, 128), BF16),
        vmem((16, 256, 128), BF16), vmem((256, 3072), BF16), vmem((16, 64, 256), BF16),
        vmem((9, 256, 256), BF16), vmem((9, 192, 256), BF16),
        vmem((8, 8, 8, 256), F32), vmem((512, 256), F32), vmem((256, 512), BF16), vmem((8, 8, 8, 256), F32),
        vmem((10, 16, 1280), BF16), vmem((2, 8, 1024), F32), vmem((2, 8, 1280), F32),
        vmem((2, 2, 8, 128), F32), vmem((2, 2, 3, 8, 128), F32), vmem((2, 16, 1280), F32),
        vmem((2, 16, 1152), F32), vmem((9, 10, 2, 24, 128), F32), vmem((4, 8, 512), BF16),
        vmem((9, 64, 256), F32),
        vmem((2048, 128), F32), vmem((1024, 128), F32), vmem((2048, 128), BF16), vmem((1024, 128), BF16),
        vmem((2048, 128), BF16), vmem((1024, 128), BF16),
        vmem((1024, 128), BF16), vmem((1024, 128), BF16), vmem((group - 1, up_piece, 128), BF16),
        vmem((row_group, up_piece, 128), BF16),
        vmem((512, 128), BF16), vmem((512, 128), BF16), vmem((group - 1, cv_piece, 128), BF16),
        vmem((row_group, cv_piece, 128), BF16),
        dma((8,)), dma((2,)), dma((2,)), dma((2, 5)), dma((2, 5)),
    ]
    coarse, fin_up, fin_conv = pl.pallas_call(
        functools.partial(main_kernel, sizes),
        name="halo_compute_reduce",
        out_shape=(
            jax.ShapeDtypeStruct((4, 8, 512), BF16),
            jax.ShapeDtypeStruct((2048, 128), BF16),
            jax.ShapeDtypeStruct((1024, 128), BF16),
        ),
        in_specs=[anywhere] * 4,
        out_specs=(anywhere,) * 3,
        scratch_shapes=scratch,
        compiler_params=pltpu.CompilerParams(
            collective_id=0, has_side_effects=True, vmem_limit_bytes=60 * 2**20
        ),
    )(coarse_in, out_grad, up_weight, conv_weight)
    return pl.pallas_call(
        functools.partial(last_kernel, 1.0 / math.sqrt(every_cell)),
        name="scale_outputs",
        out_shape=(
            jax.ShapeDtypeStruct((4, 8, 512), BF16),
            jax.ShapeDtypeStruct((64, C, C), F32),
            jax.ShapeDtypeStruct((27, C, C), F32),
        ),
        in_specs=[anywhere] * 3,
        out_specs=(anywhere,) * 3,
        scratch_shapes=[
            vmem((2048, 128), BF16), vmem((1024, 128), BF16), vmem((64, C, C), F32), vmem((27, C, C), F32),
            dma((5,)), dma((6,)),
        ],
        compiler_params=pltpu.CompilerParams(vmem_limit_bytes=60 * 2**20),
    )(coarse, fin_up, fin_conv)


def solution(mesh):
    sizes = tuple(mesh.shape[a] for a in ("gx", "gy", "gz"))
    in_specs = (P("gx", "gy", "gz"), P("gx", "gy", "gz"), P(), P())
    out_specs = (P("gx", "gy", "gz"), P(), P())
    return jax.shard_map(
        functools.partial(local, sizes), mesh=mesh, in_specs=in_specs, out_specs=out_specs, check_vma=False
    )
```

```python
import functools
import itertools
import math

import jax
import jax.numpy as jnp
from jax import lax
from jax.experimental import pallas as pl
from jax.experimental.pallas import tpu as pltpu
from jax.sharding import PartitionSpec as P

MESH = pl.DeviceIdType.MESH
F32 = jnp.float32
BF16 = jnp.bfloat16
C = 64
gelu_coef = 0.7978845608
gelu_cube = 0.044715
taps_by_parity = (((0, 3), (1, 1)), ((1, 2), (2, 0)))
NEIGHBOURS = sorted((o for o in itertools.product((-1, 0, 1), repeat=3) if any(o)), key=lambda o: (-abs(o[0]), sum(map(abs, o))))
G_PLANES = [0, 3, 4, 5, 6, 7, 8, 9, 12, 15]
U_PLANES = [1, 2, 10, 11, 13, 14]


def nt(left, right):
    return lax.dot_general(left, right, (((1,), (1,)), ((), ())), preferred_element_type=F32)


def nn(left, right):
    return jnp.dot(left, right, preferred_element_type=F32)


class Place:
    def __init__(self, sizes):
        self.sizes = sizes
        self.gx, self.gy, self.gz = (lax.axis_index(a) for a in ("gx", "gy", "gz"))
        self.nz, self.nx, self.ny = sizes[0] // 2, sizes[1], sizes[2]
        self.low = sizes[2] // 2
        self.z, self.x = self.gx // 2, self.gy
        self.y = self.gx % 2 * self.low + self.gz // 2
        self.core = self.gz % 2
        self.index = self.z * self.nx + self.x
        self.group = self.nz * self.nx
        self.row_group = 2 * self.low

    def neighbour(self, o):
        me = (self.gx, self.gy, self.gz)
        return tuple(lax.rem(m + d + n, n) for m, d, n in zip(me, o, self.sizes))

    def sibling(self):
        return (self.gx, self.gy, self.gz + 1 - 2 * self.core)

    def in_group(self, dz, dx):
        z, x = lax.rem(self.z + dz, self.nz), lax.rem(self.x + dx, self.nx)
        return (z * 2 + self.gx % 2, x, self.gz), z * self.nx + x

    def in_row(self, dy):
        y = lax.rem(self.y + dy, self.row_group)
        return (self.z * 2 + y // self.low, self.x, y % self.low * 2 + self.core)

    def group_steps(self):
        far = lambda o: -min(o[0], self.nz - o[0]) - min(o[1], self.nx - o[1])
        return sorted((o for o in itertools.product(range(self.nz), range(self.nx)) if any(o)), key=far)


def remote(src, dst, send, recv, device):
    return pltpu.make_async_remote_copy(
        src_ref=src, dst_ref=dst, send_sem=send, recv_sem=recv, device_id=device, device_id_type=MESH
    )


def await_bytes(ref, sem):
    pltpu.make_async_copy(ref, ref, sem).wait()


def halo(place, xt, edge, faces, extra, ys, yt, ct, ctr, sems):
    copies = []
    planes, lanes = xt.shape[0], xt.shape[2] - 256
    inner = planes - 2 * edge
    for ox, oy, oz in NEIGHBOURS:
        device = place.neighbour((ox, oy, oz))
        zs, zd = {
            0: (pl.ds(0, lanes), pl.ds(128, lanes)),
            1: (pl.ds(lanes - 128, 128), pl.ds(0, 128)),
            -1: (pl.ds(0, 128), pl.ds(lanes + 128, 128)),
        }[oz]
        side, end = (1 - oy) // 2, (1 - ox) // 2
        if oy == 0:
            zs = pl.ds(zs.start + 128, zs.size)
            if ox == 0:
                xs, xd = pl.ds(edge, inner), pl.ds(edge, inner)
            elif oz == 0:
                xs, xd = faces[end]
            else:
                xs, xd = (
                    (pl.ds(inner, edge), pl.ds(0, edge)),
                    (pl.ds(edge, edge), pl.ds(planes - edge, edge)),
                )[end]
            src, dst = xt.at[xs, :, zs], xt.at[xd, :, zd]
        elif ox == 0:
            src, dst = ys.at[side, :, zs], yt.at[side, :, zd]
        else:
            src, dst = ct.at[end, side], ctr.at[end, side, 1 - oz]
        copies.append((src, dst, device))
        if extra is not None and ox != 0 and (oy, oz) == (0, 0):
            source, target = extra
            copies.append((source.at[end], target.at[end], device))
    for src, dst, device in copies:
        remote(src, dst, sems.at[0], sems.at[1], device).start()
    return sum(math.prod(src.shape) * jnp.dtype(src.dtype).itemsize for src, _, _ in copies)


class AllReduce:
    def __init__(self, place, total, rounded, fin, r1, s, r2, r3, sems):
        self.place, self.total, self.rounded, self.fin = place, total, rounded, fin
        self.r1, self.s, self.r2, self.r3, self.sems = r1, s, r2, r3, sems
        self.half = total.shape[0] // 2
        self.piece = self.half // place.group
        self.step = -1
        self.sizes = (r1, r2, r3.at[pl.ds(0, place.row_group - 1)], r2, s)

    def send(self, src, dst, device):
        remote(src, dst, self.sems.at[0, self.step], self.sems.at[1, self.step], device).start()

    def arrive(self):
        await_bytes(self.sizes[self.step], self.sems.at[1, self.step])
        self.step += 1

    def finish(self):
        self.arrive()
        self.store.wait()
        for step, size in enumerate(self.sizes):
            await_bytes(size, self.sems.at[0, step])

    def mine(self, index, size):
        return pl.ds(pl.multiple_of(index * size, size), size)

    def pair(self, part=0, parts=1):
        p = self.place
        self.step = 0
        size = self.half // parts
        rows = pl.ds(pl.multiple_of((1 - p.core) * self.half + part * size, size), size)
        self.send(self.rounded.at[rows], self.r1.at[pl.ds(part * size, size)], p.sibling())

    def scatter(self):
        p = self.place
        self.arrive()
        self.s[...] = (self.total[self.mine(p.core, self.half), :] + self.r1[...].astype(F32)).astype(BF16)
        for k, o in enumerate(p.group_steps()):
            device, index = p.in_group(*o)
            self.send(self.s.at[self.mine(index, self.piece)], self.r2.at[k], device)

    def exchange(self):
        p = self.place
        self.arrive()
        total = self.s[self.mine(p.index, self.piece), :].astype(F32)
        for k in range(p.group - 1):
            total = total + self.r2[k].astype(F32)
        self.r3[p.y] = total.astype(BF16)
        for dy in sorted(range(1, p.row_group), key=lambda d: -min(d, p.row_group - d)):
            self.send(self.r3.at[p.y], self.r3.at[p.y], p.in_row(dy))

    def spot(self):
        p = self.place
        return pl.ds(pl.multiple_of(p.core * self.half + p.index * self.piece, self.piece), self.piece)

    def gather(self):
        p = self.place
        self.arrive()
        total = self.r3[0].astype(F32)
        for k in range(1, p.row_group):
            total = total + self.r3[k].astype(F32)
        self.fin[self.spot(), :] = total.astype(BF16)
        for o in p.group_steps():
            device, _ = p.in_group(*o)
            self.send(self.fin.at[self.spot()], self.fin.at[self.spot()], device)

    def share(self, out, sem):
        p = self.place
        self.arrive()
        spot = self.mine(p.core, self.half)
        self.send(self.fin.at[spot], out.at[spot], p.sibling())
        self.store = pltpu.make_async_copy(self.fin.at[spot], out.at[spot], sem)
        self.store.start()


def main_kernel(
    sizes, u_in, g_in, wu_in, wc_in,
    coarse_out, out_up, out_conv,
    ub, wu, wc, ue, ue1, uc, uce, xt, ysf, ys, yt, ct, ctr, ctf, yf, yr, ge, ga, gb,
    wp, cw, w3, uw, uwt, pre, slope, ht, gp,
    pxt, pys, pyt, pct, pctr, pyf, pyr, pe, co, gc,
    a_up, a_conv, b_up, b_conv, fin_up, fin_conv, up_r1, up_s, up_r2, up_r3, cv_r1, cv_s, cv_r2, cv_r3,
    local_sems, g_sems, p_sems, up_sems, cv_sems,
):
    place = Place(sizes)
    barrier = pltpu.get_barrier_semaphore()
    partners = [place.neighbour(o) for o in NEIGHBOURS]
    partners += [place.in_group(*o)[0] for o in place.group_steps()]
    partners += [place.in_row(dy) for dy in range(1, place.row_group)]
    partners += [place.sibling()]
    for device in partners[:26]:
        pl.semaphore_signal(barrier, inc=1, device_id=device, device_id_type=MESH)
    loads = [
        pltpu.make_async_copy(u_in, ub, local_sems.at[0]),
        pltpu.make_async_copy(g_in.at[pl.ds(0, 7)], xt.at[pl.ds(3, 7), :, pl.ds(128, 1024)], local_sems.at[1]),
        pltpu.make_async_copy(g_in.at[7], xt.at[12, :, pl.ds(128, 1024)], local_sems.at[2]),
        pltpu.make_async_copy(wu_in, wu, local_sems.at[3]),
        pltpu.make_async_copy(wc_in, wc, local_sems.at[4]),
    ]
    for load in loads:
        load.start()
    for device in partners[26:]:
        pl.semaphore_signal(barrier, inc=1, device_id=device, device_id_type=MESH)

    zero_rows = jnp.zeros((4, 1024), F32)
    for side in range(2):
        ysf[side, 12:16, :] = zero_rows
    loads[0].wait()
    for x in range(4):
        rows = ub[x].astype(F32)
        ue[1 + x, 8:16, 128:640] = rows
        plane = U_PLANES[1 + x]
        for z, lane in ((0, 128), (384, 1024)):
            both = jnp.concatenate([rows[:, z : z + 128], rows[:, z : z + 128]], axis=0)
            xt[plane, :, lane : lane + 128] = both.astype(BF16)
        if x in (0, 3):
            uc[(3 - x) // 3] = jnp.concatenate([rows[:, 0:256], rows[:, 256:512]], axis=0).astype(BF16)
        for side, row in ((0, 7), (1, 0)):
            ysf[side, 8 + x : 9 + x, 0:256] = rows[row : row + 1, 0:256]
            ysf[side, 8 + x : 9 + x, 256:768] = jnp.zeros((1, 512), F32)
            ysf[side, 8 + x : 9 + x, 768:1024] = rows[row : row + 1, 256:512]
    loads[1].wait()
    loads[2].wait()
    for x in range(8):
        block = xt[G_PLANES[1 + x], :, 128:1152].astype(F32)
        ysf[0, x : x + 1, :] = block[15:16]
        ysf[1, x : x + 1, :] = block[0:1]
    for side in range(2):
        ys[side] = ysf[side].astype(BF16)
        for end, x, xc in ((0, 7, 3), (1, 0, 0)):
            ctf[end, side, 0, 8:16, :] = jnp.zeros((8, 128), F32)
            for j in range(8):
                ctf[end, side, 0, j : j + 1, :] = ysf[side, x : x + 1, 128 * j : 128 * j + 128]
            for j, lane in enumerate((0, 128, 768, 896)):
                ctf[end, side, 0, 8 + j : 9 + j, :] = ysf[side, 8 + xc : 9 + xc, lane : lane + 128]
            ct[end, side] = ctf[end, side, 0].astype(BF16)
    pl.semaphore_wait(barrier, len(partners))
    rim_bytes = halo(place, xt, 2, ((12, 0), (3, 15)), (uc, uce), ys, yt, ct, ctr, g_sems)

    loads[3].wait()
    loads[4].wait()
    blank = jnp.zeros((C, C), BF16)
    for q in range(16):
        k0, k1, k2, k3 = (wu[4 * q + k] for k in range(4))
        wp[q, 0:64, :] = jnp.concatenate([k3, blank], axis=1)
        wp[q, 64:128, :] = jnp.concatenate([k1, k2], axis=1)
        wp[q, 128:192, :] = jnp.concatenate([blank, k0], axis=1)
        wp[q, 192:256, :] = jnp.zeros((C, 2 * C), BF16)
        w3[q, :, 0:128] = jnp.concatenate([k0, k1], axis=1)
        w3[q, :, 128:256] = jnp.concatenate([k2, k3], axis=1)
    for dx in range(3):
        for dy in range(3):
            d0, d1, d2 = (wc[9 * dx + 3 * dy + d] for d in range(3))
            tap = jnp.concatenate(
                [
                    jnp.concatenate([d2, d1, d0, blank], axis=1),
                    jnp.concatenate([blank, d2, d1, d0], axis=1),
                ],
                axis=0,
            )
            for py in range(2):
                lane = 256 * (4 * dx + py - dy + 2)
                cw[128 * py : 128 * py + 128, lane : lane + 256] = tap
        cw[128:256, 1024 * dx : 1024 * dx + 256] = jnp.zeros((128, 256), BF16)
        cw[0:128, 1024 * dx + 768 : 1024 * dx + 1024] = jnp.zeros((128, 256), BF16)

    await_bytes(slope.at[pl.ds(0, rim_bytes // 1024)], g_sems.at[1])
    ctf[...] = ctr[...].astype(F32)
    for side in range(2):
        yf[side, 0:16, :] = yt[side].astype(F32)
        for end in range(2):
            for j in range(10):
                tile, row = (0, 7) if j == 0 else (2, 0) if j == 9 else (1, j - 1)
                yf[side, 16 + end : 17 + end, 128 * j : 128 * j + 128] = ctf[end, side, tile, row : row + 1, :]
            for j in range(6):
                tile, row = (0, 11) if j == 0 else (2, 8) if j == 5 else (1, 7 + j)
                ue[5 * end, 7 + 9 * side : 8 + 9 * side, 128 * j : 128 * j + 128] = ctf[
                    end, side, tile, row : row + 1, :
                ]
        for x in range(1, 5):
            row = slice(7 + x, 8 + x)
            ue[x, 7 + 9 * side : 8 + 9 * side, 0:384] = yf[side, row, 0:384]
            ue[x, 7 + 9 * side : 8 + 9 * side, 384:768] = yf[side, row, 896:1280]
    for end in range(2):
        face = uce[end].astype(F32)
        ue[5 * end, 8:16, 128:384] = face[0:8]
        ue[5 * end, 8:16, 384:640] = face[8:16]
    for x in range(6):
        ue[x, 8:16, 0:128] = xt[U_PLANES[x], :, 0:128].astype(F32)[0:8]
        ue[x, 8:16, 640:768] = xt[U_PLANES[x], :, 1152:1280].astype(F32)[0:8]
    for x in range(6):
        ue1[x] = pltpu.roll(ue[x], 768 - 64, 1)[:, :640]
    for sx in range(3):
        for sy in range(3):
            rows = []
            for zc in range(8):
                if zc % 2:
                    part = ue[sx : sx + 4, 7 + sy : 15 + sy, 64 * (zc + 1) : 64 * (zc + 1) + 256]
                else:
                    part = ue1[sx : sx + 4, 7 + sy : 15 + sy, 64 * zc : 64 * zc + 256]
                rows.append(part.reshape(32, 256))
            window = jnp.concatenate(rows, axis=0)
            uw[3 * sx + sy] = window.astype(BF16)
            uwt[3 * sx + sy] = window.T.astype(BF16)[:192]

    for px in range(2):
        for py in range(2):
            total = None
            for sx, kx in taps_by_parity[px]:
                for sy, ky in taps_by_parity[py]:
                    part = nn(uw[3 * sx + sy], wp[4 * kx + ky])
                    total = part if total is None else total + part
            total = total.reshape(8, 4, 8, 128)
            for xc in range(4):
                pre[:, 2 * xc + px, :, 128 * py : 128 * py + 128] = total[:, xc]
    for zc in range(0, 8, 2):
        v = pre[zc : zc + 2].reshape(128, 256)
        square = v * v
        gate = 0.5 + 0.5 * jnp.tanh(v * (gelu_coef + gelu_coef * gelu_cube * square))
        hidden = v * gate
        ht[:, 64 * zc : 64 * zc + 128] = hidden.T.astype(BF16)
        slope[64 * zc : 64 * zc + 128, :] = gate + hidden * (1.0 - gate) * (
            2.0 * gelu_coef + 6.0 * gelu_coef * gelu_cube * square
        )

    turn = xt.shape[2] - 64
    for side in range(2):
        yr[side] = pltpu.roll(yf[side], turn, 1)[:, :1152]
    for x in range(10):
        turned = pltpu.roll(xt[G_PLANES[x]].astype(F32), turn, 1)
        row = 16 if x == 0 else 17 if x == 9 else x - 1
        for pair in range(9):
            lanes = slice(128 * pair, 128 * pair + 128)
            ge[pair, x, 8:24, :] = turned[:, lanes]
            ge[pair, x, 7:8, :] = yr[0, row : row + 1, lanes]
            ge[pair, x, 24:25, :] = yr[1, row : row + 1, lanes]
    for pair in range(9):
        for ky in range(4):
            rows = [ge[pair, x, pl.ds(7 + ky, 8, stride=2), :] for x in range(10)]
            ga[ky, pair] = jnp.concatenate(rows, axis=0).astype(BF16)
            gb[ky, pair] = jnp.concatenate(rows[1:9], axis=0).astype(BF16)

    def window(dx, ky):
        parts = []
        for zc in range(8):
            if dx == 1:
                pairs = [gb[ky, zc + s] for s in range(2)]
            else:
                first = 16 - 8 * dx
                pairs = [ga[ky, zc + s, first : first + 64] for s in range(2)]
            parts.append(jnp.concatenate(pairs, axis=1))
        return jnp.concatenate(parts, axis=0)

    low = lax.broadcasted_iota(jnp.int32, (C, 2 * C), 1) < C
    for dx in range(3):
        products = [
            nn(ht[0:128, :], window(dx, 0)),
            nn(ht[...], window(dx, 1)),
            nn(ht[...], window(dx, 2)),
            nn(ht[128:256, :], window(dx, 3)),
        ]
        for dy in range(3):
            part = products[2 - dy][:128] + products[3 - dy][-128:]
            gc[3 * dx + dy] = part[:64] + pltpu.roll(part[64:], 256 - 64, 1)
    for t in range(9):
        a_conv[64 * t : 64 * t + 64, :] = gc[t, :, 0:128]
    for m in range(5):
        if m < 4:
            other = pltpu.roll(gc[2 * m + 1, :, 128:256], 64, 1)
            joined = jnp.where(low, gc[2 * m, :, 128:256], other)
        else:
            joined = gc[8, :, 128:256]
        a_conv[64 * (9 + m) : 64 * (10 + m), :] = joined
    a_conv[896:1024, :] = jnp.zeros((128, 128), F32)
    b_conv[...] = a_conv[...].astype(BF16)
    conv = AllReduce(place, a_conv, b_conv, fin_conv, cv_r1, cv_s, cv_r2, cv_r3, cv_sems)
    conv.pair()

    total = None
    for dx in range(3):
        for ky in range(4):
            lane = 256 * (4 * dx + ky)
            part = nt(window(dx, ky), cw[:, lane : lane + 256])
            total = part if total is None else total + part
    gp[...] = (total * slope[...]).astype(BF16).astype(F32).reshape(8, 8, 8, 256)

    conv.scatter()

    up = AllReduce(place, a_up, b_up, fin_up, up_r1, up_s, up_r2, up_r3, up_sems)
    for px in range(2):
        rows = [gp[:, 2 * xc + px, :, :] for xc in range(4)]
        grad = jnp.stack(rows, axis=1).reshape(256, 256).astype(BF16)
        for i, (sx, _) in enumerate(taps_by_parity[px]):
            product = nn(uwt[3 * sx : 3 * sx + 3].reshape(576, 256), grad)
            for py in range(2):
                for j, (sy, _) in enumerate(taps_by_parity[py]):
                    row = 1024 * i + 512 * px + 256 * py + 128 * j
                    first = 192 * sy
                    part = product[first : first + 192, 128 * py : 128 * py + 128]
                    outer = jnp.where(low, part[0:64], part[128:192])
                    a_up[row : row + 64, :] = part[64:128]
                    a_up[row + 64 : row + 128, :] = outer
                    b_up[row : row + 64, :] = part[64:128].astype(BF16)
                    b_up[row + 64 : row + 128, :] = outer.astype(BF16)
        up.pair(px, 2)

    for x in range(8):
        for zc in range(8):
            block = gp[zc, x]
            rows = jnp.concatenate([block[:, 0:128], block[:, 128:256]], axis=0)
            pxt[1 + x, :, 128 * zc + 128 : 128 * zc + 256] = rows.astype(BF16)
            pys[0, x : x + 1, 128 * zc : 128 * zc + 128] = gp[zc, x, 7:8, 128:256]
            pys[1, x : x + 1, 128 * zc : 128 * zc + 128] = gp[zc, x, 0:1, 0:128]
            if x in (0, 7):
                pct[(7 - x) // 7, 0, zc : zc + 1, :] = gp[zc, x, 7:8, 128:256]
                pct[(7 - x) // 7, 1, zc : zc + 1, :] = gp[zc, x, 0:1, 0:128]
    up.scatter()
    conv.exchange()
    p_bytes = halo(place, pxt, 1, ((8, 0), (1, 9)), None, pys, pyt, pct, pctr, p_sems)
    up.exchange()
    conv.gather()
    up.gather()

    await_bytes(slope.at[pl.ds(0, p_bytes // 1024)], p_sems.at[1])
    for side in range(2):
        pyf[side, 0:8, :] = pyt[side]
        for end in range(2):
            for j in range(10):
                tile, row = (0, 7) if j == 0 else (2, 0) if j == 9 else (1, j - 1)
                pyf[side, 8 + end : 9 + end, 128 * j : 128 * j + 128] = pctr[end, side, tile, row : row + 1, :]
        pyr[side] = pltpu.roll(pyf[side], turn, 1)[:, :1152]
    for x in range(10):
        turned = pltpu.roll(pxt[x].astype(F32), turn, 1)
        row = 8 if x == 0 else 9 if x == 9 else x - 1
        for pair in range(9):
            lanes = slice(128 * pair, 128 * pair + 128)
            pe[pair, x, 0, 8:16, :] = turned[0:8, lanes]
            pe[pair, x, 1, 8:16, :] = turned[8:16, lanes]
            pe[pair, x, 0, 16:17, :] = pyr[1, row : row + 1, lanes]
            pe[pair, x, 1, 7:8, :] = pyr[0, row : row + 1, lanes]
    total = None
    for kx in range(4):
        for ky in range(4):
            parity, first = ((1, 7), (0, 8), (1, 8), (0, 9))[ky]
            pairs = [
                jnp.concatenate([pe[pair, 2 * xc + kx, parity, first : first + 8, :] for xc in range(4)], axis=0)
                for pair in range(9)
            ]
            rows = [jnp.concatenate([pairs[zc], pairs[zc + 1]], axis=1) for zc in range(8)]
            part = nt(jnp.concatenate(rows, axis=0).astype(BF16), w3[4 * kx + ky])
            total = part if total is None else total + part
    total = total.reshape(8, 4, 8, C)
    for zc in range(0, 8, 2):
        co[:, :, 64 * zc : 64 * zc + 128] = jnp.concatenate([total[zc], total[zc + 1]], axis=2).astype(BF16)
    store = pltpu.make_async_copy(co, coarse_out, local_sems.at[5])
    store.start()
    conv.share(out_conv, local_sems.at[6])
    up.share(out_up, local_sems.at[7])
    up.finish()
    conv.finish()
    store.wait()
    await_bytes(slope.at[pl.ds(0, rim_bytes // 1024)], g_sems.at[0])
    await_bytes(slope.at[pl.ds(0, p_bytes // 1024)], p_sems.at[0])


def last_kernel(
    factor, coarse, in_up, in_conv, coarse_out, up_out, conv_out, fin_up, fin_conv, up, conv, in_sems, out_sems
):
    through = pltpu.make_async_copy(coarse, coarse_out, out_sems.at[5])
    through.start()
    parts = [pl.ds(512 * i, 512) for i in range(4)]
    loads = [pltpu.make_async_copy(in_up.at[p], fin_up.at[p], in_sems.at[i]) for i, p in enumerate(parts)]
    loads.append(pltpu.make_async_copy(in_conv, fin_conv, in_sems.at[4]))
    for load in loads:
        load.start()
    stores = []
    for i in range(4):
        loads[i].wait()
        for s in range(4 * i, 4 * i + 4):
            half, px, py, j = s // 8, s // 4 % 2, s // 2 % 2, s % 2
            q = 4 * taps_by_parity[px][half][1] + taps_by_parity[py][j][1]
            first = fin_up[128 * s : 128 * s + 64, :].astype(F32) * factor
            second = fin_up[128 * s + 64 : 128 * s + 128, :].astype(F32) * factor
            up[4 * q + 1] = first[:, :C]
            up[4 * q + 2] = first[:, C:]
            up[4 * q + 3] = second[:, :C]
            up[4 * q] = second[:, C:]
        kx = taps_by_parity[i % 2][i // 2][1]
        part = pl.ds(16 * kx, 16)
        stores.append(pltpu.make_async_copy(up.at[part], up_out.at[part], out_sems.at[i]))
        stores[-1].start()
    loads[4].wait()
    for t in range(9):
        both = fin_conv[64 * t : 64 * t + 64, :].astype(F32) * factor
        conv[3 * t + 2] = both[:, :C]
        conv[3 * t + 1] = both[:, C:]
        m = t // 2
        rest = fin_conv[64 * (9 + m) : 64 * (10 + m), :].astype(F32) * factor
        conv[3 * t] = rest[:, C:] if t % 2 else rest[:, :C]
    stores.append(pltpu.make_async_copy(conv, conv_out, out_sems.at[4]))
    stores[-1].start()
    for store in stores:
        store.wait()
    through.wait()


def local(sizes, coarse_in, out_grad, up_weight, conv_weight):
    every_cell = 2048 * sizes[0] * sizes[1] * sizes[2]
    group = sizes[0] // 2 * sizes[1]
    row_group = sizes[2] // 2 * 2
    up_piece, cv_piece = 1024 // group, 512 // group
    vmem = pltpu.VMEM
    dma = pltpu.SemaphoreType.DMA
    anywhere = pl.BlockSpec(memory_space=pl.ANY)
    scratch = [
        vmem((4, 8, 512), BF16), vmem((64, C, C), BF16), vmem((27, C, C), BF16),
        vmem((6, 24, 768), F32), vmem((6, 24, 640), F32), vmem((2, 16, 256), BF16), vmem((2, 16, 256), BF16),
        vmem((16, 16, 1280), BF16), vmem((2, 16, 1024), F32), vmem((2, 16, 1024), BF16),
        vmem((2, 16, 1280), BF16), vmem((2, 2, 16, 128), BF16), vmem((2, 2, 3, 16, 128), BF16),
        vmem((2, 2, 3, 16, 128), F32), vmem((2, 24, 1280), F32), vmem((2, 24, 1152), F32),
        vmem((9, 10, 32, 128), F32), vmem((4, 9, 80, 128), BF16), vmem((4, 9, 64, 128), BF16),
        vmem((16, 256, 128), BF16), vmem((256, 3072), BF16), vmem((16, 64, 256), BF16),
        vmem((9, 256, 256), BF16), vmem((9, 192, 256), BF16),
        vmem((8, 8, 8, 256), F32), vmem((512, 256), F32), vmem((256, 512), BF16), vmem((8, 8, 8, 256), F32),
        vmem((10, 16, 1280), BF16), vmem((2, 8, 1024), F32), vmem((2, 8, 1280), F32),
        vmem((2, 2, 8, 128), F32), vmem((2, 2, 3, 8, 128), F32), vmem((2, 16, 1280), F32),
        vmem((2, 16, 1152), F32), vmem((9, 10, 2, 24, 128), F32), vmem((4, 8, 512), BF16),
        vmem((9, 64, 256), F32),
        vmem((2048, 128), F32), vmem((1024, 128), F32), vmem((2048, 128), BF16), vmem((1024, 128), BF16),
        vmem((2048, 128), BF16), vmem((1024, 128), BF16),
        vmem((1024, 128), BF16), vmem((1024, 128), BF16), vmem((group - 1, up_piece, 128), BF16),
        vmem((row_group, up_piece, 128), BF16),
        vmem((512, 128), BF16), vmem((512, 128), BF16), vmem((group - 1, cv_piece, 128), BF16),
        vmem((row_group, cv_piece, 128), BF16),
        dma((8,)), dma((2,)), dma((2,)), dma((2, 5)), dma((2, 5)),
    ]
    coarse, fin_up, fin_conv = pl.pallas_call(
        functools.partial(main_kernel, sizes),
        name="halo_compute_reduce",
        out_shape=(
            jax.ShapeDtypeStruct((4, 8, 512), BF16),
            jax.ShapeDtypeStruct((2048, 128), BF16),
            jax.ShapeDtypeStruct((1024, 128), BF16),
        ),
        in_specs=[anywhere] * 4,
        out_specs=(anywhere,) * 3,
        scratch_shapes=scratch,
        compiler_params=pltpu.CompilerParams(
            collective_id=0, has_side_effects=True, vmem_limit_bytes=60 * 2**20
        ),
    )(coarse_in, out_grad, up_weight, conv_weight)
    return pl.pallas_call(
        functools.partial(last_kernel, 1.0 / math.sqrt(every_cell)),
        name="scale_outputs",
        out_shape=(
            jax.ShapeDtypeStruct((4, 8, 512), BF16),
            jax.ShapeDtypeStruct((64, C, C), F32),
            jax.ShapeDtypeStruct((27, C, C), F32),
        ),
        in_specs=[anywhere] * 3,
        out_specs=(anywhere,) * 3,
        scratch_shapes=[
            vmem((2048, 128), BF16), vmem((1024, 128), BF16), vmem((64, C, C), F32), vmem((27, C, C), F32),
            dma((5,)), dma((6,)),
        ],
        compiler_params=pltpu.CompilerParams(vmem_limit_bytes=60 * 2**20),
    )(coarse, fin_up, fin_conv)


def solution(mesh):
    sizes = tuple(mesh.shape[a] for a in ("gx", "gy", "gz"))
    in_specs = (P("gx", "gy", "gz"), P("gx", "gy", "gz"), P(), P())
    out_specs = (P("gx", "gy", "gz"), P(), P())
    return jax.shard_map(
        functools.partial(local, sizes), mesh=mesh, in_specs=in_specs, out_specs=out_specs, check_vma=False
    )
```
